256 devices in a mesh: blk: 16 (over z, x_hi), dp: 16 (over x_lo, y, core).
Axes of the slice: x: 4 (x_hi: 2, x_lo: 2; x = x_hi * 2 + x_lo), y: 4, z: 8, core: 2. Of those that a mesh axis runs over, the one named last changes fastest.
Arguments:
- score_feats: bfloat16 [16, 3840, 1024], P('dp', 'blk'), may hold values from -6 to 6
- audio_feats: bfloat16 [16, 3840, 1024], P('dp', 'blk'), may hold values from -6 to 6
- score_weight: bfloat16 [1024, 1024], replicated, may hold values from -0.1875 to 0.1875
- audio_weight: bfloat16 [1024, 1024], replicated, may hold values from -0.1875 to 0.1875
- log_temp: float32 [1], replicated, may hold values from 1.6 to 3
- logit_bias: float32 [1], replicated, may hold values from -3 to -1
- loss_scale: float32 [1], replicated, may hold values from 150000 to 400000
Outputs:
- score_feat_grad: bfloat16 [16, 3840, 1024], P('dp', 'blk')
- audio_feat_grad: bfloat16 [16, 3840, 1024], P('dp', 'blk')
- score_weight_grad: float32 [1024, 1024], P('blk')
- audio_weight_grad: float32 [1024, 1024], P('blk')
The draws below stay inside these ranges and needn't reach their ends.
All inputs are finite; a program needn't handle non-finite values.
Results may differ from the reference program's by a relative error of at most 0.023.
Values may be sent and summed in bfloat16 or wider, within the bound.
A program may use at most 128 MiB of HBM per device.

```python
import math
import jax
import jax.numpy as jnp
from jax import lax

D = 1024
E = 1024
ROWS = 3840
GROUPS = 16


def spiked(values, rng, source, target, blocks, factor):
    def block_of(axis_at):
        return (jnp.arange(values.shape[axis_at]) // (values.shape[axis_at] // blocks)).reshape((-1,) + (1,) * (values.ndim - 1 - axis_at))

    one_side = jax.random.permutation(rng, blocks)[block_of(target)]
    second = (block_of(target) + blocks // 2) % blocks
    return jnp.where((block_of(source) == one_side) | (block_of(source) == second), factor * values, values)


def steps_of(stream_key, dims, split, least, top_value):
    loudness, own = 1.0, jax.random.fold_in(stream_key, 6)
    for axis_at, shards_of in split:
        draws = jnp.exp(jax.random.uniform(jax.random.fold_in(own, axis_at), (shards_of,), jnp.float32, least / len(split), top_value / len(split)))
        loudness = loudness * jnp.repeat(draws, dims[axis_at] // shards_of).reshape([-1 if axis == axis_at else 1 for axis in range(len(dims))])
    return loudness


def gaussian(key, shape, width, reach, cuts=(), kind=jnp.bfloat16):
    result = jax.random.normal(key, shape, jnp.float32) * width
    if len(cuts) > 0:
        result = steps_of(key, shape, cuts, -0.22, 0.18) * result
    return jnp.clip(result, min=-reach, max=reach).astype(kind)


def heavy_noise(key, extent, width, most, pieces, heavy, kind=jnp.bfloat16):
    array = width * jax.random.normal(key, extent, jnp.float32)
    if pieces:
        array = array * steps_of(key, extent, pieces, -0.22, 0.18)
    return jnp.clip(spiked(array, jax.random.fold_in(key, 3), *heavy), -most, most).astype(kind)


def setup_inputs(seed: int = 0) -> dict:
    streams_of = jax.random.split(jax.random.key(seed), 8)
    score_feats = heavy_noise(streams_of[0], (GROUPS, ROWS, D), 1.0, 6.0, ((0, 16), (1, 16)), (1, 2, 16, 2.0))
    audio_feats = heavy_noise(streams_of[1], (GROUPS, ROWS, D), 1.0, 6.0, ((0, 16), (1, 16)), (1, 2, 16, 2.0))
    score_weight = gaussian(streams_of[2], (D, E), D ** -0.5, 0.1875)
    audio_weight = gaussian(streams_of[3], (D, E), D ** -0.5, 0.1875)
    log_temp = jnp.clip(jax.random.uniform(streams_of[4], (1,), jnp.float32, 1.6, 3.0), 1.6, 3.0)
    logit_bias = jnp.clip(jax.random.uniform(streams_of[5], (1,), jnp.float32, -3.0, -1.0), -3.0, -1.0)
    loss_scale = jnp.clip(jnp.exp(jax.random.uniform(streams_of[6], (1,), jnp.float32, math.log(150000.0), math.log(400000.0))), 150000.0, 400000.0)
    return dict(score_feats=score_feats, audio_feats=audio_feats, score_weight=score_weight, audio_weight=audio_weight, log_temp=log_temp, logit_bias=logit_bias, loss_scale=loss_scale)


def tower_forward(features, weights):
    projected = jnp.dot(features, weights, preferred_element_type=jnp.float32)
    norm_vals = jnp.sqrt(lax.optimization_barrier(jnp.sum(projected * projected, axis=-1, keepdims=True)) + 1e-06)
    return (projected / norm_vals, norm_vals)

def unit_grad(unit_vec, norm_vals, grad_emb):
    radial = lax.optimization_barrier(jnp.sum(unit_vec * grad_emb, axis=-1, keepdims=True))
    return ((grad_emb - unit_vec * radial) / norm_vals).astype(jnp.bfloat16)

def reference(score_feats, audio_feats, score_weight, audio_weight, log_temp, logit_bias, loss_scale):
    group_total = score_feats.shape[0]
    row_total = score_feats.shape[1]
    temper = jnp.exp(log_temp[0])
    factor = loss_scale[0] * temper / (group_total * row_total)

    def group_step(running, inputs_pair):
        score_feat, audio_feat = inputs_pair
        score_unit, score_len = tower_forward(score_feat, score_weight)
        audio_unit, audio_len = tower_forward(audio_feat, audio_weight)
        score_emb = score_unit.astype(jnp.bfloat16)
        audio_emb = audio_unit.astype(jnp.bfloat16)
        similarity = jnp.dot(score_emb, audio_emb.T, preferred_element_type=jnp.float32)
        logits = temper * similarity + logit_bias[0]
        row_ids = lax.broadcasted_iota(jnp.int32, logits.shape, 0)
        col_ids = lax.broadcasted_iota(jnp.int32, logits.shape, 1)
        targets = (row_ids == col_ids).astype(logits.dtype)
        logit_grad = (jax.nn.sigmoid(logits) - targets).astype(jnp.bfloat16)
        score_emb_grad = factor * jnp.dot(logit_grad, audio_emb, preferred_element_type=jnp.float32)
        audio_emb_grad = factor * jnp.dot(logit_grad.T, score_emb, preferred_element_type=jnp.float32)
        score_proj_grad = unit_grad(score_unit, score_len, score_emb_grad)
        audio_proj_grad = unit_grad(audio_unit, audio_len, audio_emb_grad)
        score_back = jnp.dot(score_proj_grad, score_weight.T, preferred_element_type=jnp.float32).astype(jnp.bfloat16)
        audio_back = jnp.dot(audio_proj_grad, audio_weight.T, preferred_element_type=jnp.float32).astype(jnp.bfloat16)
        score_wsum = running[0] + jnp.dot(score_feat.T, score_proj_grad, preferred_element_type=jnp.float32)
        audio_wsum = running[1] + jnp.dot(audio_feat.T, audio_proj_grad, preferred_element_type=jnp.float32)
        return ((score_wsum, audio_wsum), (score_back, audio_back))
    zero_grad = jnp.zeros(score_weight.shape, jnp.float32)
    sums, backs = lax.scan(group_step, (zero_grad, zero_grad), (score_feats, audio_feats))
    return (backs[0], backs[1], sums[0], sums[1])
```

```python
import functools

import jax
import jax.numpy as jnp
from jax import lax
from jax.experimental import pallas as pl
from jax.experimental.pallas import tpu as pltpu
from jax.sharding import PartitionSpec as P

MESH = pl.DeviceIdType.MESH
BF = jnp.bfloat16
F32 = jnp.float32
ROWS = 240
WIDTH = 1024
TILE = 256
STEP = 48

LOW = ((0, 64), (64, 48))
HIGH = ((112, 64), (176, 64))
CHUNKS = LOW + HIGH
PLUS, MINUS = 0, 1
GATHER_FAR = {PLUS: HIGH, MINUS: LOW}
SUM_FAR = {PLUS: LOW, MINUS: HIGH}


def dot_nn(a, b):
    return lax.dot_general(a, b, (((1,), (0,)), ((), ())), preferred_element_type=F32)


def dot_nt(a, b):
    return lax.dot_general(a, b, (((1,), (1,)), ((), ())), preferred_element_type=F32)


def dot_tn(a, b):
    return lax.dot_general(a, b, (((0,), (0,)), ((), ())), preferred_element_type=F32)


def tile_at(index, size):
    return pl.ds(pl.multiple_of(index * size, size), size)


def kernel(
    groups_rows,
    feat_s, feat_a, weight_s, weight_a, temp_ref, bias_ref, scale_ref,
    back_s, back_a, rows_s, rows_a,
    unit, length, audio, score, grad_t, part, ring, side_out, side_in, emb_grad, proj_grad,
    outer, core_in, half, y_in, x_in, y_sum, x_sum, x_in2, y_in2, z_out, z_in, done,
    gather_send, gather_recv, ring_send, ring_recv, side_send, side_recv,
    core_send, core_recv, one_send, one_recv, two_send, two_recv, z_send, z_recv, all_send, all_recv,
):
    blk, dp = lax.axis_index("blk"), lax.axis_index("dp")
    zz, xh = blk // 2, lax.rem(blk, 2)
    xl, yy, core = dp // 8, lax.rem(dp // 2, 4), lax.rem(dp, 2)
    xx = xh * 2 + xl

    def device(dx=0, dy=0, dz=0, dc=0):
        x = lax.rem(xx + dx, 4)
        y = lax.rem(yy + dy, 4)
        z = lax.rem(zz + dz, 8)
        c = lax.rem(core + dc, 2)
        return {"blk": z * 2 + x // 2, "dp": (lax.rem(x, 2) * 4 + y) * 2 + c}

    def flat_dp(offset):
        return {"blk": blk, "dp": lax.rem(dp + offset, 16)}

    def remote(src, dst, send, recv, target):
        return pltpu.make_async_remote_copy(
            src_ref=src, dst_ref=dst, send_sem=send, recv_sem=recv, device_id=target, device_id_type=MESH
        )

    barrier = pltpu.get_barrier_semaphore()
    peers = [device(dz=k) for k in range(1, 8)] + [flat_dp(k) for k in range(1, 16)]
    peers += [device(dx=k) for k in (1, 2, 3)]
    for peer in peers:
        pl.semaphore_signal(barrier, inc=1, device_id=peer, device_id_type=MESH)

    temper = jnp.exp(jnp.full((1, 1), temp_ref[0], F32))
    bias = bias_ref[0]
    factor = scale_ref[0] * temper / groups_rows

    pending = []

    def launch(copy):
        copy.start()
        pending.append(copy)

    def rows_in(first, count, fn):
        def step(i, carry):
            fn(pl.ds(pl.multiple_of(first + i * 16, 16), 16))
            return carry

        lax.fori_loop(0, count // 16, step, 0, unroll=True)

    def project(tower, feat, weight, store):
        def column(j, carry):
            cols = tile_at(j, TILE)
            unit[tower, :, cols] = dot_nn(feat[...], weight[:, cols])
            return carry

        lax.fori_loop(0, WIDTH // TILE, column, 0)

        def scale(i, carry):
            rows = tile_at(i, STEP)
            value = unit[tower, rows, :]
            norm = jnp.sqrt(jnp.sum(value * value, axis=-1, keepdims=True) + 1e-06)
            value = value / norm
            unit[tower, rows, :] = value
            length[tower, rows, :] = jnp.broadcast_to(norm, (STEP, 128))
            store(rows, value.astype(BF))
            return carry

        lax.fori_loop(0, ROWS // STEP, scale, 0)

    def store_audio(rows, value):
        audio[0, rows, :] = value

    def store_score(rows, value):
        score[0, rows, :] = value

    def gather_copy(way, hop, chunk):
        first, count = chunk
        rows = pl.ds(first, count)
        if way == PLUS:
            here, there = (8 - (hop - 1)) % 8, 8 - hop
        else:
            here, there = hop - 1, hop
        index = CHUNKS.index(chunk)
        return remote(
            audio.at[here, rows], audio.at[there, rows],
            gather_send.at[way, hop - 1, index], gather_recv.at[way, hop - 1, index],
            device(dz=1 if way == PLUS else 7),
        )

    def ring_slot(way, ahead):
        return ahead if way == PLUS else (8 - ahead) % 8

    def ring_copy(way, hop, chunk):
        first, count = chunk
        rows = pl.ds(first, count)
        start = 0 if chunk in SUM_FAR[way] else 1
        src = part.at[ring_slot(way, 4 - hop), rows] if hop == start else ring.at[way, hop - 1, rows]
        index = CHUNKS.index(chunk)
        return remote(
            src, ring.at[way, hop, rows],
            ring_send.at[way, hop, index], ring_recv.at[way, hop, index],
            device(dz=1 if way == PLUS else 7),
        )

    def ring_take(way, hop, chunk):
        ring_copy(way, hop, chunk).wait_recv()
        if hop < 3:
            slot = ring_slot(way, 3 - hop)

            def add(rows):
                ring[way, hop, rows, :] = (
                    ring[way, hop, rows, :].astype(F32) + part[slot, rows, :].astype(F32)
                ).astype(BF)

            rows_in(chunk[0], chunk[1], add)
            launch(ring_copy(way, hop + 1, chunk))

    def tile_grads(slot, own):
        for side in range(2):
            logits = temper * dot_nt(audio[slot], score[side]) + bias
            grads = jax.nn.sigmoid(logits)
            if own and side == 0:
                row_ids = lax.broadcasted_iota(jnp.int32, (ROWS, ROWS), 0)
                col_ids = lax.broadcasted_iota(jnp.int32, (ROWS, ROWS), 1)
                grads = grads - (row_ids == col_ids).astype(F32)
            grad_t[side, slot] = grads.astype(BF)

        def column(j, carry):
            cols = tile_at(j, TILE)
            part[slot, :, cols] = (
                dot_nn(grad_t[0, slot], score[0, :, cols]) + dot_nn(grad_t[1, slot], score[1, :, cols])
            ).astype(BF)
            return carry

        lax.fori_loop(0, WIDTH // TILE, column, 0)

    def tile_pair(hop):
        def one(i, carry):
            tile_grads(hop + i * (8 - 2 * hop), False)
            return carry

        lax.fori_loop(0, 2, one, 0)

    def score_grad(side, store):
        def column(j, carry):
            cols = tile_at(j, TILE)
            total = dot_tn(grad_t[side, 0], audio[0, :, cols])
            for slot in range(1, 8):
                total += dot_tn(grad_t[side, slot], audio[slot, :, cols])
            store(cols, total)
            return carry

        lax.fori_loop(0, WIDTH // TILE, column, 0)

    def unit_grad(tower, value_of):
        def step(i, carry):
            rows = pl.ds(pl.multiple_of(i * 16, 16), 16)
            grad = factor * value_of(rows)
            vec = unit[tower, rows, :]
            radial = jnp.sum(vec * grad, axis=-1, keepdims=True)
            norm = length[tower, rows, 0:1]
            proj_grad[tower, rows, :] = ((grad - vec * radial) / norm).astype(BF)
            return carry

        lax.fori_loop(0, ROWS // 16, step, 0)

    def back(tower, weight, out):
        def column(j, carry):
            cols = tile_at(j, TILE)
            out[:, cols] = dot_nt(proj_grad[tower], weight[cols, :]).astype(BF)
            return carry

        lax.fori_loop(0, WIDTH // TILE, column, 0)

    def weight_part(tower, feat, owner):
        def step(z, carry):
            for j in range(2):
                cols = pl.ds(pl.multiple_of(owner * 512 + j * 256, 256), 256)
                value = dot_tn(feat[:, tile_at(z, 128)], proj_grad[tower, :, cols]).astype(BF)
                for q in range(2):
                    for x in range(4):
                        for route in range(2):
                            first = x * 32 + route * 16
                            outer[tower, owner * 4 + j * 2 + q, route, x, z] = value[
                                first : first + 16, q * 128 : q * 128 + 128
                            ]
            return carry

        lax.fori_loop(0, 8, step, 0)

    def core_copy(tower):
        other = lax.rem(core + 1, 2)
        return remote(
            outer.at[tower, pl.ds(other * 4, 4)], core_in.at[tower],
            core_send.at[tower], core_recv.at[tower], device(dc=1),
        )

    def one_copies(tower):
        copies = []
        for k in (2, 1, 3):
            copies.append(remote(
                half.at[tower, lax.rem(yy + k, 4), 0], y_in.at[tower, k - 1],
                one_send.at[tower, 0, k - 1], one_recv.at[tower, 0, k - 1], device(dy=k),
            ))
            copies.append(remote(
                half.at[tower, :, 1, lax.rem(xx + k, 4)], x_in.at[tower, k - 1],
                one_send.at[tower, 1, k - 1], one_recv.at[tower, 1, k - 1], device(dx=k),
            ))
        return copies

    def two_copies(tower):
        copies = []
        for k in (2, 1, 3):
            copies.append(remote(
                y_sum.at[tower, lax.rem(xx + k, 4)], x_in2.at[tower, k - 1],
                two_send.at[tower, 0, k - 1], two_recv.at[tower, 0, k - 1], device(dx=k),
            ))
            copies.append(remote(
                x_sum.at[tower, lax.rem(yy + k, 4)], y_in2.at[tower, k - 1],
                two_send.at[tower, 1, k - 1], two_recv.at[tower, 1, k - 1], device(dy=k),
            ))
        return copies

    def z_copies(tower):
        return [
            remote(
                z_out.at[tower, lax.rem(zz + k, 8)], z_in.at[tower, k - 1],
                z_send.at[tower, k - 1], z_recv.at[tower, k - 1], device(dz=k),
            )
            for k in (4, 3, 5, 2, 6, 1, 7)
        ]

    place_q = core * 4 + yy

    def all_copies(tower):
        return [
            remote(
                done.at[tower, place_q, xl], done.at[tower, place_q, xl],
                all_send.at[tower, k - 1], all_recv.at[tower, k - 1], flat_dp(k),
            )
            for k in range(1, 16)
        ]

    def stage_core_sum(tower):
        core_copy(tower).wait_recv()

        def step(i, carry):
            y = i // 4
            x = lax.rem(i, 4)
            for route in range(2):
                half[tower, y, route, x] = (
                    outer[tower, core * 4 + y, route, x].astype(F32) + core_in[tower, y, route, x].astype(F32)
                ).astype(BF)
            return carry

        lax.fori_loop(0, 16, step, 0)
        for copy in one_copies(tower):
            launch(copy)

    def stage_one_sum(tower):
        for copy in one_copies(tower):
            copy.wait_recv()

        def step(i, carry):
            total = half[tower, yy, 0, i].astype(F32)
            for k in range(3):
                total += y_in[tower, k, i].astype(F32)
            y_sum[tower, i] = total.astype(BF)
            total = half[tower, i, 1, xx].astype(F32)
            for k in range(3):
                total += x_in[tower, k, i].astype(F32)
            x_sum[tower, i] = total.astype(BF)
            return carry

        lax.fori_loop(0, 4, step, 0)
        for copy in two_copies(tower):
            launch(copy)

    def stage_two_sum(tower):
        for copy in two_copies(tower):
            copy.wait_recv()
        total = y_sum[tower, xx].astype(F32)
        for k in range(3):
            total += x_in2[tower, k].astype(F32)
        z_out[tower, :, 0] = total.astype(BF)
        total = x_sum[tower, yy].astype(F32)
        for k in range(3):
            total += y_in2[tower, k].astype(F32)
        z_out[tower, :, 1] = total.astype(BF)
        for copy in z_copies(tower):
            launch(copy)

    def stage_z_sum(tower):
        for copy in z_copies(tower):
            copy.wait_recv()
        total = z_out[tower, zz].astype(F32)
        for k in range(7):
            total += z_in[tower, k].astype(F32)
        done[tower, place_q, xl] = total.astype(BF)
        for copy in all_copies(tower):
            launch(copy)

    def stage_all(tower, out):
        for copy in all_copies(tower):
            copy.wait_recv()
        for q in range(8):
            for half_rows in range(2):
                for route in range(2):
                    first = half_rows * 32 + route * 16
                    out[first : first + 16, q * 128 : q * 128 + 128] = done[tower, q, half_rows, route]

    project(1, feat_a, weight_a, store_audio)
    pl.semaphore_wait(barrier, len(peers))
    for chunk in CHUNKS:
        for way in (PLUS, MINUS):
            launch(gather_copy(way, 1, chunk))
    project(0, feat_s, weight_s, store_score)
    pair = remote(score.at[0], score.at[1], side_send.at[0], side_recv.at[0], device(dx=2))
    launch(pair)

    for hop in range(1, 5):
        for chunk in CHUNKS:
            for way in (PLUS, MINUS):
                if hop == 4 and chunk not in GATHER_FAR[way]:
                    continue
                gather_copy(way, hop, chunk).wait_recv()
                if hop < 3 or (hop == 3 and chunk in GATHER_FAR[way]):
                    launch(gather_copy(way, hop + 1, chunk))
        if hop == 1:
            pair.wait_recv()
            tile_grads(0, True)
        if hop < 4:
            tile_pair(hop)
        else:
            tile_grads(4, False)
        if hop >= 3:
            for way in (PLUS, MINUS):
                for chunk in SUM_FAR[way] if hop == 4 else SUM_FAR[1 - way]:
                    launch(ring_copy(way, 4 - hop, chunk))

    def store_side(cols, value):
        side_out[:, cols] = value.astype(BF)

    def store_own(cols, value):
        emb_grad[:, cols] = value

    def near(hop):
        for k in range(2):
            for way in (PLUS, MINUS):
                ring_take(way, hop, SUM_FAR[1 - way][k])

    def far(hop):
        for k in range(2):
            for way in (PLUS, MINUS):
                ring_take(way, hop, SUM_FAR[way][k])

    score_grad(1, store_side)
    side = remote(side_out, side_in, side_send.at[1], side_recv.at[1], device(dx=2))
    launch(side)
    near(1)
    score_grad(0, store_own)
    far(0)
    near(2)
    side.wait_recv()
    unit_grad(0, lambda rows: emb_grad[rows, :] + side_in[rows, :].astype(F32))
    weight_part(0, feat_s, lax.rem(core + 1, 2))
    launch(core_copy(0))
    far(1)
    weight_part(0, feat_s, core)
    stage_core_sum(0)
    back(0, weight_s, back_s)
    near(3)
    far(2)
    stage_one_sum(0)
    stage_two_sum(0)
    far(3)

    def audio_value(rows):
        return (
            part[0, rows, :].astype(F32) + ring[PLUS, 3, rows, :].astype(F32) + ring[MINUS, 3, rows, :].astype(F32)
        )

    unit_grad(1, audio_value)
    weight_part(1, feat_a, lax.rem(core + 1, 2))
    launch(core_copy(1))
    weight_part(1, feat_a, core)
    stage_core_sum(1)
    back(1, weight_a, back_a)
    stage_z_sum(0)
    stage_one_sum(1)
    stage_all(0, rows_s)
    stage_two_sum(1)
    stage_z_sum(1)
    stage_all(1, rows_a)
    for copy in pending:
        copy.wait_send()


def body(score_feats, audio_feats, score_weight, audio_weight, log_temp, logit_bias, loss_scale):
    groups_rows = float(lax.axis_size("dp") * lax.axis_size("blk") * score_feats.shape[1])
    vmem = pl.BlockSpec(memory_space=pltpu.VMEM)
    smem = pl.BlockSpec(memory_space=pltpu.SMEM)
    rows = jax.ShapeDtypeStruct((ROWS, WIDTH), BF)
    sums = jax.ShapeDtypeStruct((64, WIDTH), BF)
    dma = pltpu.SemaphoreType.DMA
    scratch = [
        pltpu.VMEM((2, ROWS, WIDTH), F32),
        pltpu.VMEM((2, ROWS, 128), F32),
        pltpu.VMEM((8, ROWS, WIDTH), BF),
        pltpu.VMEM((2, ROWS, WIDTH), BF),
        pltpu.VMEM((2, 8, ROWS, ROWS), BF),
        pltpu.VMEM((8, ROWS, WIDTH), BF),
        pltpu.VMEM((2, 4, ROWS, WIDTH), BF),
        pltpu.VMEM((ROWS, WIDTH), BF),
        pltpu.VMEM((ROWS, WIDTH), BF),
        pltpu.VMEM((ROWS, WIDTH), F32),
        pltpu.VMEM((2, ROWS, WIDTH), BF),
        pltpu.VMEM((2, 8, 2, 4, 8, 16, 128), BF),
        pltpu.VMEM((2, 4, 2, 4, 8, 16, 128), BF),
        pltpu.VMEM((2, 4, 2, 4, 8, 16, 128), BF),
        pltpu.VMEM((2, 3, 4, 8, 16, 128), BF),
        pltpu.VMEM((2, 3, 4, 8, 16, 128), BF),
        pltpu.VMEM((2, 4, 8, 16, 128), BF),
        pltpu.VMEM((2, 4, 8, 16, 128), BF),
        pltpu.VMEM((2, 3, 8, 16, 128), BF),
        pltpu.VMEM((2, 3, 8, 16, 128), BF),
        pltpu.VMEM((2, 8, 2, 16, 128), BF),
        pltpu.VMEM((2, 7, 2, 16, 128), BF),
        pltpu.VMEM((2, 8, 2, 2, 16, 128), BF),
        dma((2, 4, 4)),
        dma((2, 4, 4)),
        dma((2, 4, 4)),
        dma((2, 4, 4)),
        dma((2,)),
        dma((2,)),
        dma((2,)),
        dma((2,)),
        dma((2, 2, 3)),
        dma((2, 2, 3)),
        dma((2, 2, 3)),
        dma((2, 2, 3)),
        dma((2, 7)),
        dma((2, 7)),
        dma((2, 15)),
        dma((2, 15)),
    ]
    back_s, back_a, rows_s, rows_a = pl.pallas_call(
        functools.partial(kernel, groups_rows),
        out_shape=(rows, rows, sums, sums),
        in_specs=[vmem] * 4 + [smem] * 3,
        out_specs=(vmem,) * 4,
        scratch_shapes=scratch,
        compiler_params=pltpu.CompilerParams(
            collective_id=0, has_side_effects=True, vmem_limit_bytes=58 * 2**20
        ),
    )(score_feats[0], audio_feats[0], score_weight, audio_weight, log_temp, logit_bias, loss_scale)
    return back_s[None], back_a[None], rows_s.astype(F32), rows_a.astype(F32)


def solution(mesh):
    in_specs = (P("dp", "blk", None), P("dp", "blk", None), P(), P(), P(), P(), P())
    out_specs = (P("dp", "blk", None), P("dp", "blk", None), P("blk", None), P("blk", None))
    return jax.shard_map(body, mesh=mesh, in_specs=in_specs, out_specs=out_specs, check_vma=False)
```

```python
import functools

import jax
import jax.numpy as jnp
from jax import lax
from jax.experimental import pallas as pl
from jax.experimental.pallas import tpu as pltpu
from jax.sharding import PartitionSpec as P

MESH = pl.DeviceIdType.MESH
BF = jnp.bfloat16
F32 = jnp.float32
ROWS = 240
WIDTH = 1024
TILE = 256
STEP = 48

LOW = ((0, 64), (64, 48))
HIGH = ((112, 64), (176, 64))
CHUNKS = LOW + HIGH
PLUS, MINUS = 0, 1
GATHER_FAR = {PLUS: HIGH, MINUS: LOW}
SUM_FAR = {PLUS: LOW, MINUS: HIGH}


def dot_nn(a, b):
    return lax.dot_general(a, b, (((1,), (0,)), ((), ())), preferred_element_type=F32)


def dot_nt(a, b):
    return lax.dot_general(a, b, (((1,), (1,)), ((), ())), preferred_element_type=F32)


def dot_tn(a, b):
    return lax.dot_general(a, b, (((0,), (0,)), ((), ())), preferred_element_type=F32)


def tile_at(index, size):
    return pl.ds(pl.multiple_of(index * size, size), size)


def kernel(
    groups_rows,
    feat_s_in, feat_a_in, weight_s_in, weight_a_in, temp_in, bias_in, scale_in,
    back_s_out, back_a_out, rows_s_out, rows_a_out,
    feat_s, feat_a, weight_s, weight_a, temp_ref, bias_ref, scale_ref,
    back_s, back_a, rows_s, rows_a, feat_t,
    load_sem, save_sem,
    unit, length, audio, score, grad_t, part, ring, side_out, side_in, emb_grad, proj_grad,
    outer, core_in, half, y_in, x_in, y_sum, x_sum, x_in2, y_in2, z_out, z_in, done,
    gather_send, gather_recv, ring_send, ring_recv, side_send, side_recv,
    core_send, core_recv, one_send, one_recv, two_send, two_recv, z_send, z_recv, all_send, all_recv,
):
    blk, dp = lax.axis_index("blk"), lax.axis_index("dp")
    zz, xh = blk // 2, lax.rem(blk, 2)
    xl, yy, core = dp // 8, lax.rem(dp // 2, 4), lax.rem(dp, 2)
    xx = xh * 2 + xl

    def device(dx=0, dy=0, dz=0, dc=0):
        x = lax.rem(xx + dx, 4)
        y = lax.rem(yy + dy, 4)
        z = lax.rem(zz + dz, 8)
        c = lax.rem(core + dc, 2)
        return {"blk": z * 2 + x // 2, "dp": (lax.rem(x, 2) * 4 + y) * 2 + c}

    def flat_dp(offset):
        return {"blk": blk, "dp": lax.rem(dp + offset, 16)}

    def remote(src, dst, send, recv, target):
        return pltpu.make_async_remote_copy(
            src_ref=src, dst_ref=dst, send_sem=send, recv_sem=recv, device_id=target, device_id_type=MESH
        )

    barrier = pltpu.get_barrier_semaphore()
    peers = [device(dz=k) for k in range(1, 8)] + [flat_dp(k) for k in range(1, 16)]
    peers += [device(dx=k) for k in (1, 2, 3)]
    for peer in peers:
        pl.semaphore_signal(barrier, inc=1, device_id=peer, device_id_type=MESH)

    loads = [
        pltpu.make_async_copy(src, dst, load_sem.at[i])
        for i, (src, dst) in enumerate((
            (feat_a_in, feat_a), (weight_a_in, weight_a), (feat_s_in, feat_s), (weight_s_in, weight_s),
            (temp_in, temp_ref), (bias_in, bias_ref), (scale_in, scale_ref),
        ))
    ]
    for copy in loads:
        copy.start()
    for copy in loads[4:]:
        copy.wait()

    temper = jnp.exp(jnp.full((1, 1), temp_ref[0], F32))
    bias = bias_ref[0]
    factor = scale_ref[0] * temper / groups_rows

    def launch(copy):
        copy.start()

    def launch_all(copies):
        for copy in copies:
            copy.start()

    def rows_in(first, count, fn):
        def step(i, carry):
            fn(pl.ds(pl.multiple_of(first + i * 16, 16), 16))
            return carry

        lax.fori_loop(0, count // 16, step, 0, unroll=True)

    def project(tower, feat, weight, store):
        def column(j, carry):
            cols = tile_at(j, TILE)
            unit[tower, :, cols] = dot_nn(feat[...], weight[:, cols])
            return carry

        lax.fori_loop(0, WIDTH // TILE, column, 0)

        def scale(i, carry):
            rows = tile_at(i, STEP)
            value = unit[tower, rows, :]
            norm = jnp.sqrt(jnp.sum(value * value, axis=-1, keepdims=True) + 1e-06)
            value = value / norm
            unit[tower, rows, :] = value
            length[tower, rows, :] = jnp.broadcast_to(norm, (STEP, 128))
            store(rows, value.astype(BF))
            return carry

        lax.fori_loop(0, ROWS // STEP, scale, 0)

    def store_audio(rows, value):
        audio[0, rows, :] = value

    def store_score(rows, value):
        score[0, rows, :] = value

    def gather_copy(way, hop, chunk):
        first, count = chunk
        rows = pl.ds(first, count)
        if way == PLUS:
            here, there = (8 - (hop - 1)) % 8, 8 - hop
        else:
            here, there = hop - 1, hop
        index = CHUNKS.index(chunk)
        return remote(
            audio.at[here, rows], audio.at[there, rows],
            gather_send.at[way, hop - 1], gather_recv.at[way, hop - 1, index],
            device(dz=1 if way == PLUS else 7),
        )

    def ring_slot(way, ahead):
        return ahead if way == PLUS else (8 - ahead) % 8

    def ring_copy(way, hop, chunk):
        first, count = chunk
        rows = pl.ds(first, count)
        start = 0 if chunk in SUM_FAR[way] else 1
        src = part.at[ring_slot(way, 4 - hop), rows] if hop == start else ring.at[way, hop - 1, rows]
        index = CHUNKS.index(chunk)
        return remote(
            src, ring.at[way, hop, rows],
            ring_send.at[way, hop], ring_recv.at[way, hop, index],
            device(dz=1 if way == PLUS else 7),
        )

    def ring_take(way, hop, chunk):
        ring_copy(way, hop, chunk).wait_recv()
        if hop < 3:
            slot = ring_slot(way, 3 - hop)

            def add(rows):
                ring[way, hop, rows, :] = (
                    ring[way, hop, rows, :].astype(F32) + part[slot, rows, :].astype(F32)
                ).astype(BF)

            rows_in(chunk[0], chunk[1], add)
            launch(ring_copy(way, hop + 1, chunk))

    def tile_grads(slot, own):
        for side in range(2):
            logits = temper * dot_nt(audio[slot], score[side]) + bias
            grads = jax.nn.sigmoid(logits)
            if own and side == 0:
                row_ids = lax.broadcasted_iota(jnp.int32, (ROWS, ROWS), 0)
                col_ids = lax.broadcasted_iota(jnp.int32, (ROWS, ROWS), 1)
                grads = grads - (row_ids == col_ids).astype(F32)
            grad_t[side, slot] = grads.astype(BF)

        def column(j, carry):
            cols = tile_at(j, TILE)
            part[slot, :, cols] = (
                dot_nn(grad_t[0, slot], score[0, :, cols]) + dot_nn(grad_t[1, slot], score[1, :, cols])
            ).astype(BF)
            return carry

        lax.fori_loop(0, WIDTH // TILE, column, 0)

    def tile_pair(hop):
        def one(i, carry):
            tile_grads(hop + i * (8 - 2 * hop), False)
            return carry

        lax.fori_loop(0, 2, one, 0)

    def score_grad(side, store):
        def column(j, carry):
            cols = tile_at(j, TILE)
            total = dot_tn(grad_t[side, 0], audio[0, :, cols])
            for slot in range(1, 8):
                total += dot_tn(grad_t[side, slot], audio[slot, :, cols])
            store(cols, total)
            return carry

        lax.fori_loop(0, WIDTH // TILE, column, 0)

    def unit_grad(tower, value_of, first, count):
        def step(rows):
            grad = factor * value_of(rows)
            vec = unit[tower, rows, :]
            radial = jnp.sum(vec * grad, axis=-1, keepdims=True)
            norm = length[tower, rows, 0:1]
            proj_grad[tower, rows, :] = ((grad - vec * radial) / norm).astype(BF)

        rows_in(first, count, step)

    def back(tower, weight, out):
        def column(j, carry):
            cols = tile_at(j, TILE)
            out[:, cols] = dot_nt(proj_grad[tower], weight[cols, :]).astype(BF)
            return carry

        lax.fori_loop(0, WIDTH // TILE, column, 0)

    def transpose(tower, feat):
        def step(z, carry):
            cols = tile_at(z, 128)
            feat_t[tower, cols, :] = feat[:, cols].T
            return carry

        lax.fori_loop(0, 8, step, 0)

    def core_pair(order):
        return lax.rem(yy // 2 + 1 + order, 2)

    def weight_part(tower, owner, order):
        pair = core_pair(order)
        cols = tile_at(owner * 2 + pair, 256)

        def step(z, carry):
            value = dot_nn(feat_t[tower, tile_at(z, 128), :], proj_grad[tower, :, cols]).astype(BF)
            for q in range(2):
                for x in range(4):
                    for route in range(2):
                        first = x * 32 + route * 16
                        outer[tower, owner * 4 + pair * 2 + q, route, x, z] = value[
                            first : first + 16, q * 128 : q * 128 + 128
                        ]
            return carry

        lax.fori_loop(0, 8, step, 0)

    def core_copy(tower, order):
        other = lax.rem(core + 1, 2)
        pair = core_pair(order)
        return remote(
            outer.at[tower, pl.ds(other * 4 + pair * 2, 2)], core_in.at[tower, pl.ds(pair * 2, 2)],
            core_send.at[tower, order], core_recv.at[tower, order], device(dc=1),
        )

    def weight_other(tower):
        for order in range(2):
            weight_part(tower, lax.rem(core + 1, 2), order)
            launch(core_copy(tower, order))

    def weight_own(tower):
        for order in range(2):
            weight_part(tower, core, order)

    def one_copies(tower):
        copies = []
        for k in (2, 1, 3):
            copies.append(remote(
                half.at[tower, lax.rem(yy + k, 4), 0], y_in.at[tower, k - 1],
                one_send.at[tower, 0], one_recv.at[tower, 0], device(dy=k),
            ))
            copies.append(remote(
                half.at[tower, :, 1, lax.rem(xx + k, 4)], x_in.at[tower, k - 1],
                one_send.at[tower, 1], one_recv.at[tower, 1], device(dx=k),
            ))
        return copies

    def two_copies(tower):
        copies = []
        for k in (2, 1, 3):
            copies.append(remote(
                y_sum.at[tower, lax.rem(xx + k, 4)], x_in2.at[tower, k - 1],
                two_send.at[tower, 0], two_recv.at[tower, 0], device(dx=k),
            ))
            copies.append(remote(
                x_sum.at[tower, lax.rem(yy + k, 4)], y_in2.at[tower, k - 1],
                two_send.at[tower, 1], two_recv.at[tower, 1], device(dy=k),
            ))
        return copies

    def z_copies(tower):
        return [
            remote(
                z_out.at[tower, lax.rem(zz + k, 8)], z_in.at[tower, k - 1],
                z_send.at[tower, 0], z_recv.at[tower, 0], device(dz=k),
            )
            for k in (4, 3, 5, 2, 6, 1, 7)
        ]

    place = (core * 4 + yy) * 2 + xl

    def all_copies(tower):
        return [
            remote(
                done.at[tower, place], done.at[tower, place],
                all_send.at[tower, 0], all_recv.at[tower, 0], flat_dp(k),
            )
            for k in range(1, 16)
        ]

    def stage_waits(tower, name):
        bufs, send, recv = {
            "one": ((y_in, x_in), one_send, one_recv),
            "two": ((x_in2, y_in2), two_send, two_recv),
            "z": ((z_in,), z_send, z_recv),
            "all": ((done,), all_send, all_recv),
        }[name]
        copies = []
        for i, buf in enumerate(bufs):
            view = buf.at[tower, pl.ds(0, 15)] if name == "all" else buf.at[tower]
            copies.append(remote(view, view, send.at[tower, i], recv.at[tower, i], device(dc=1)))
        return copies

    def stage_core_sum(tower, order):
        pair = core_pair(order)
        core_copy(tower, order).wait_recv()

        def step(i, carry):
            y = pair * 2 + i // 4
            x = lax.rem(i, 4)
            for route in range(2):
                half[tower, y, route, x] = (
                    outer[tower, core * 4 + y, route, x].astype(F32) + core_in[tower, y, route, x].astype(F32)
                ).astype(BF)
            return carry

        lax.fori_loop(0, 8, step, 0)
        if order == 1:
            launch_all(one_copies(tower))

    def stage_one_sum(tower):
        for copy in stage_waits(tower, "one"):
            copy.wait_recv()

        def step(i, carry):
            total = half[tower, yy, 0, i].astype(F32)
            for k in range(3):
                total += y_in[tower, k, i].astype(F32)
            y_sum[tower, i] = total.astype(BF)
            total = half[tower, i, 1, xx].astype(F32)
            for k in range(3):
                total += x_in[tower, k, i].astype(F32)
            x_sum[tower, i] = total.astype(BF)
            return carry

        lax.fori_loop(0, 4, step, 0)
        launch_all(two_copies(tower))

    def stage_two_sum(tower):
        for copy in stage_waits(tower, "two"):
            copy.wait_recv()
        total = y_sum[tower, xx].astype(F32)
        for k in range(3):
            total += x_in2[tower, k].astype(F32)
        z_out[tower, :, 0] = total.astype(BF)
        total = x_sum[tower, yy].astype(F32)
        for k in range(3):
            total += y_in2[tower, k].astype(F32)
        z_out[tower, :, 1] = total.astype(BF)
        launch_all(z_copies(tower))

    def stage_z_sum(tower):
        for copy in stage_waits(tower, "z"):
            copy.wait_recv()
        total = z_out[tower, zz].astype(F32)
        for k in range(7):
            total += z_in[tower, k].astype(F32)
        done[tower, place] = total.astype(BF)
        launch_all(all_copies(tower))

    def stage_all(tower, out):
        for copy in stage_waits(tower, "all"):
            copy.wait_recv()
        for q in range(8):
            for half_rows in range(2):
                for route in range(2):
                    first = half_rows * 32 + route * 16
                    out[first : first + 16, q * 128 : q * 128 + 128] = done[tower, q * 2 + half_rows, route].astype(F32)

    loads[0].wait()
    loads[1].wait()
    project(1, feat_a, weight_a, store_audio)
    pl.semaphore_wait(barrier, len(peers))
    for chunk in CHUNKS:
        for way in (PLUS, MINUS):
            launch(gather_copy(way, 1, chunk))
    loads[2].wait()
    loads[3].wait()
    project(0, feat_s, weight_s, store_score)
    pair = remote(score.at[0], score.at[1], side_send.at[0], side_recv.at[0], device(dx=2))
    launch(pair)
    transpose(0, feat_s)
    transpose(1, feat_a)

    for hop in range(1, 5):
        for chunk in CHUNKS:
            for way in (PLUS, MINUS):
                if hop == 4 and chunk not in GATHER_FAR[way]:
                    continue
                gather_copy(way, hop, chunk).wait_recv()
                if hop < 3 or (hop == 3 and chunk in GATHER_FAR[way]):
                    launch(gather_copy(way, hop + 1, chunk))
        if hop == 1:
            pair.wait_recv()
            tile_grads(0, True)
        if hop < 4:
            tile_pair(hop)
        else:
            tile_grads(4, False)
        if hop >= 3:
            for way in (PLUS, MINUS):
                for chunk in SUM_FAR[way] if hop == 4 else SUM_FAR[1 - way]:
                    launch(ring_copy(way, 4 - hop, chunk))

    def store_side(cols, value):
        side_out[:, cols] = value.astype(BF)

    def store_own(cols, value):
        emb_grad[:, cols] = value

    def near(hop):
        for k in range(2):
            for way in (PLUS, MINUS):
                ring_take(way, hop, SUM_FAR[1 - way][k])

    def far(hop):
        for k in range(2):
            for way in (PLUS, MINUS):
                ring_take(way, hop, SUM_FAR[way][k])

    score_grad(1, store_side)
    side = remote(side_out, side_in, side_send.at[1], side_recv.at[1], device(dx=2))
    launch(side)
    near(1)
    score_grad(0, store_own)
    far(0)
    near(2)
    side.wait_recv()
    unit_grad(0, lambda rows: emb_grad[rows, :] + side_in[rows, :].astype(F32), 0, ROWS)
    weight_other(0)
    far(1)
    weight_own(0)
    stage_core_sum(0, 0)
    stage_core_sum(0, 1)
    back(0, weight_s, back_s)
    saves = [
        pltpu.make_async_copy(src, dst, save_sem.at[i])
        for i, (src, dst) in enumerate(
            ((back_s, back_s_out), (back_a, back_a_out), (rows_s, rows_s_out), (rows_a, rows_a_out))
        )
    ]
    saves[0].start()
    near(3)
    far(2)
    stage_one_sum(0)
    stage_two_sum(0)

    def audio_value(rows):
        return (
            part[0, rows, :].astype(F32) + ring[PLUS, 3, rows, :].astype(F32) + ring[MINUS, 3, rows, :].astype(F32)
        )

    for k in range(2):
        for way in (PLUS, MINUS):
            ring_take(way, 3, SUM_FAR[way][k])
            unit_grad(1, audio_value, *SUM_FAR[way][k])
    weight_other(1)
    weight_own(1)
    stage_core_sum(1, 0)
    stage_core_sum(1, 1)
    back(1, weight_a, back_a)
    saves[1].start()
    stage_z_sum(0)
    stage_one_sum(1)
    stage_all(0, rows_s)
    saves[2].start()
    stage_two_sum(1)
    stage_z_sum(1)
    stage_all(1, rows_a)
    saves[3].start()

    for way in (PLUS, MINUS):
        for hop in range(4):
            for kind in range(2):
                far_rows = (GATHER_FAR, SUM_FAR)[kind][way]
                edge = hop == (3, 0)[kind]
                rows = pl.ds(far_rows[0][0], far_rows[0][1] + far_rows[1][1]) if edge else pl.ds(0, ROWS)
                buf = (audio.at[1, rows], ring.at[way, 1, rows])[kind]
                sem = (gather_send, ring_send)[kind].at[way, hop]
                remote(buf, buf, sem, (gather_recv, ring_recv)[kind].at[way, hop, 0], device(dz=1)).wait_send()
    pair.wait_send()
    side.wait_send()
    for tower in range(2):
        for order in range(2):
            core_copy(tower, order).wait_send()
        for name in ("one", "two", "z", "all"):
            for copy in stage_waits(tower, name):
                copy.wait_send()
    for copy in saves:
        copy.wait()


def finish(*refs):
    sources, targets, held, load, save = refs[:4], refs[4:8], refs[8:12], refs[12], refs[13]
    loads = [pltpu.make_async_copy(sources[i], held[i], load.at[i]) for i in range(4)]
    saves = [pltpu.make_async_copy(held[i], targets[i], save.at[i]) for i in range(4)]
    for copy in loads:
        copy.start()
    for i in range(4):
        loads[i].wait()
        saves[i].start()
    for copy in saves:
        copy.wait()


def body(score_feats, audio_feats, score_weight, audio_weight, log_temp, logit_bias, loss_scale):
    groups_rows = float(lax.axis_size("dp") * lax.axis_size("blk") * score_feats.shape[1])
    anywhere = pl.BlockSpec(memory_space=pl.ANY)
    rows = jax.ShapeDtypeStruct((ROWS, WIDTH), BF)
    sums = jax.ShapeDtypeStruct((64, WIDTH), F32)
    dma = pltpu.SemaphoreType.DMA
    scratch = [
        pltpu.VMEM((ROWS, WIDTH), BF),
        pltpu.VMEM((ROWS, WIDTH), BF),
        pltpu.VMEM((WIDTH, WIDTH), BF),
        pltpu.VMEM((WIDTH, WIDTH), BF),
        pltpu.SMEM((1,), F32),
        pltpu.SMEM((1,), F32),
        pltpu.SMEM((1,), F32),
        pltpu.VMEM((ROWS, WIDTH), BF),
        pltpu.VMEM((ROWS, WIDTH), BF),
        pltpu.VMEM((64, WIDTH), F32),
        pltpu.VMEM((64, WIDTH), F32),
        pltpu.VMEM((2, WIDTH, ROWS), BF),
        dma((7,)),
        dma((4,)),
        pltpu.VMEM((2, ROWS, WIDTH), F32),
        pltpu.VMEM((2, ROWS, 128), F32),
        pltpu.VMEM((8, ROWS, WIDTH), BF),
        pltpu.VMEM((2, ROWS, WIDTH), BF),
        pltpu.VMEM((2, 8, ROWS, ROWS), BF),
        pltpu.VMEM((8, ROWS, WIDTH), BF),
        pltpu.VMEM((2, 4, ROWS, WIDTH), BF),
        pltpu.VMEM((ROWS, WIDTH), BF),
        pltpu.VMEM((ROWS, WIDTH), BF),
        pltpu.VMEM((ROWS, WIDTH), F32),
        pltpu.VMEM((2, ROWS, WIDTH), BF),
        pltpu.VMEM((2, 8, 2, 4, 8, 16, 128), BF),
        pltpu.VMEM((2, 4, 2, 4, 8, 16, 128), BF),
        pltpu.VMEM((2, 4, 2, 4, 8, 16, 128), BF),
        pltpu.VMEM((2, 3, 4, 8, 16, 128), BF),
        pltpu.VMEM((2, 3, 4, 8, 16, 128), BF),
        pltpu.VMEM((2, 4, 8, 16, 128), BF),
        pltpu.VMEM((2, 4, 8, 16, 128), BF),
        pltpu.VMEM((2, 3, 8, 16, 128), BF),
        pltpu.VMEM((2, 3, 8, 16, 128), BF),
        pltpu.VMEM((2, 8, 2, 16, 128), BF),
        pltpu.VMEM((2, 7, 2, 16, 128), BF),
        pltpu.VMEM((2, 16, 2, 16, 128), BF),
        dma((2, 4)),
        dma((2, 4, 4)),
        dma((2, 4)),
        dma((2, 4, 4)),
        dma((2,)),
        dma((2,)),
        dma((2, 2)),
        dma((2, 2)),
        dma((2, 2)),
        dma((2, 2)),
        dma((2, 2)),
        dma((2, 2)),
        dma((2, 1)),
        dma((2, 1)),
        dma((2, 1)),
        dma((2, 1)),
    ]
    shapes = (rows, rows, sums, sums)
    results = pl.pallas_call(
        functools.partial(kernel, groups_rows),
        out_shape=shapes,
        in_specs=[anywhere] * 7,
        out_specs=(anywhere,) * 4,
        scratch_shapes=scratch,
        compiler_params=pltpu.CompilerParams(
            collective_id=0, has_side_effects=True, vmem_limit_bytes=58 * 2**20
        ),
    )(score_feats[0], audio_feats[0], score_weight, audio_weight, log_temp, logit_bias, loss_scale)
    back_s, back_a, rows_s, rows_a = pl.pallas_call(
        finish,
        out_shape=shapes,
        in_specs=[anywhere] * 4,
        out_specs=(anywhere,) * 4,
        scratch_shapes=[pltpu.VMEM(v.shape, v.dtype) for v in shapes] + [dma((4,)), dma((4,))],
    )(*results)
    return back_s[None], back_a[None], rows_s, rows_a


def solution(mesh):
    in_specs = (P("dp", "blk", None), P("dp", "blk", None), P(), P(), P(), P(), P())
    out_specs = (P("dp", "blk", None), P("dp", "blk", None), P("blk", None), P("blk", None))
    return jax.shard_map(body, mesh=mesh, in_specs=in_specs, out_specs=out_specs, check_vma=False)
```

```python
import functools

import jax
import jax.numpy as jnp
from jax import lax
from jax.experimental import pallas as pl
from jax.experimental.pallas import tpu as pltpu
from jax.sharding import PartitionSpec as P

MESH = pl.DeviceIdType.MESH
BF = jnp.bfloat16
F32 = jnp.float32
ROWS = 240
WIDTH = 1024
TILE = 256
STEP = 48

LOW = ((0, 64), (64, 48))
HIGH = ((112, 64), (176, 64))
CHUNKS = LOW + HIGH
PLUS, MINUS = 0, 1
GATHER_FAR = {PLUS: HIGH, MINUS: LOW}
SUM_FAR = {PLUS: LOW, MINUS: HIGH}


def dot_nn(a, b):
    return lax.dot_general(a, b, (((1,), (0,)), ((), ())), preferred_element_type=F32)


def dot_nt(a, b):
    return lax.dot_general(a, b, (((1,), (1,)), ((), ())), preferred_element_type=F32)


def dot_tn(a, b):
    return lax.dot_general(a, b, (((0,), (0,)), ((), ())), preferred_element_type=F32)


def tile_at(index, size):
    return pl.ds(pl.multiple_of(index * size, size), size)


def kernel(
    groups_rows,
    feat_s_in, feat_a_in, weight_s_in, weight_a_in, temp_in, bias_in, scale_in,
    back_s, back_a, rows_s, rows_a,
    feat_s, feat_a, weight_s, weight_a, temp_ref, bias_ref, scale_ref, feat_t,
    load_sem,
    unit, length, audio, score, grad_t, part, ring, side_out, side_in, emb_grad, proj_grad,
    feat_other, proj_other, half, y_in, x_in, y_sum, x_sum, x_in2, y_in2, z_out, z_in, done,
    gather_send, gather_recv, ring_send, ring_recv, side_send, side_recv,
    core_send, core_recv, one_send, one_recv, two_send, two_recv, z_send, z_recv, all_send, all_recv,
):
    blk, dp = lax.axis_index("blk"), lax.axis_index("dp")
    zz, xh = blk // 2, lax.rem(blk, 2)
    xl, yy, core = dp // 8, lax.rem(dp // 2, 4), lax.rem(dp, 2)
    xx = xh * 2 + xl

    def device(dx=0, dy=0, dz=0, dc=0):
        x = lax.rem(xx + dx, 4)
        y = lax.rem(yy + dy, 4)
        z = lax.rem(zz + dz, 8)
        c = lax.rem(core + dc, 2)
        return {"blk": z * 2 + x // 2, "dp": (lax.rem(x, 2) * 4 + y) * 2 + c}

    def flat_dp(offset):
        return {"blk": blk, "dp": lax.rem(dp + offset, 16)}

    def remote(src, dst, send, recv, target):
        return pltpu.make_async_remote_copy(
            src_ref=src, dst_ref=dst, send_sem=send, recv_sem=recv, device_id=target, device_id_type=MESH
        )

    barrier = pltpu.get_barrier_semaphore()
    peers = [device(dz=k) for k in range(1, 8)] + [flat_dp(k) for k in range(1, 16)]
    peers += [device(dx=k) for k in (1, 2, 3)]
    for peer in peers:
        pl.semaphore_signal(barrier, inc=1, device_id=peer, device_id_type=MESH)

    loads = [
        pltpu.make_async_copy(src, dst, load_sem.at[i])
        for i, (src, dst) in enumerate((
            (feat_a_in, feat_a), (weight_a_in, weight_a), (feat_s_in, feat_s), (weight_s_in, weight_s),
            (temp_in, temp_ref), (bias_in, bias_ref), (scale_in, scale_ref),
        ))
    ]
    for copy in loads:
        copy.start()
    for copy in loads[4:]:
        copy.wait()

    temper = jnp.exp(jnp.full((1, 1), temp_ref[0], F32))
    bias = bias_ref[0]
    factor = scale_ref[0] * temper / groups_rows

    def launch(copy):
        copy.start()

    def launch_all(copies):
        for copy in copies:
            copy.start()

    def rows_in(first, count, fn):
        def step(i, carry):
            fn(pl.ds(pl.multiple_of(first + i * 16, 16), 16))
            return carry

        lax.fori_loop(0, count // 16, step, 0, unroll=True)

    def project(tower, feat, weight, store):
        def column(j, carry):
            cols = tile_at(j, TILE)
            unit[tower, :, cols] = dot_nn(feat[...], weight[:, cols])
            return carry

        lax.fori_loop(0, WIDTH // TILE, column, 0)

        def scale(i, carry):
            rows = tile_at(i, STEP)
            value = unit[tower, rows, :]
            norm = jnp.sqrt(jnp.sum(value * value, axis=-1, keepdims=True) + 1e-06)
            value = value / norm
            unit[tower, rows, :] = value
            length[tower, rows, :] = jnp.broadcast_to(norm, (STEP, 128))
            store(rows, value.astype(BF))
            return carry

        lax.fori_loop(0, ROWS // STEP, scale, 0)

    def store_audio(rows, value):
        audio[0, rows, :] = value

    def store_score(rows, value):
        score[0, rows, :] = value

    def gather_copy(way, hop, chunk):
        first, count = chunk
        rows = pl.ds(first, count)
        if way == PLUS:
            here, there = (8 - (hop - 1)) % 8, 8 - hop
        else:
            here, there = hop - 1, hop
        index = CHUNKS.index(chunk)
        return remote(
            audio.at[here, rows], audio.at[there, rows],
            gather_send.at[way, hop - 1], gather_recv.at[way, hop - 1, index],
            device(dz=1 if way == PLUS else 7),
        )

    def ring_slot(way, ahead):
        return ahead if way == PLUS else (8 - ahead) % 8

    def ring_copy(way, hop, chunk):
        first, count = chunk
        rows = pl.ds(first, count)
        start = 0 if chunk in SUM_FAR[way] else 1
        src = part.at[ring_slot(way, 4 - hop), rows] if hop == start else ring.at[way, hop - 1, rows]
        index = CHUNKS.index(chunk)
        return remote(
            src, ring.at[way, hop, rows],
            ring_send.at[way, hop], ring_recv.at[way, hop, index],
            device(dz=1 if way == PLUS else 7),
        )

    def ring_take(way, hop, chunk):
        ring_copy(way, hop, chunk).wait_recv()
        if hop < 3:
            slot = ring_slot(way, 3 - hop)

            def add(rows):
                ring[way, hop, rows, :] = (
                    ring[way, hop, rows, :].astype(F32) + part[slot, rows, :].astype(F32)
                ).astype(BF)

            rows_in(chunk[0], chunk[1], add)
            launch(ring_copy(way, hop + 1, chunk))

    def tile_grads(slot, own):
        for side in range(2):
            logits = temper * dot_nt(audio[slot], score[side]) + bias
            grads = jax.nn.sigmoid(logits)
            if own and side == 0:
                row_ids = lax.broadcasted_iota(jnp.int32, (ROWS, ROWS), 0)
                col_ids = lax.broadcasted_iota(jnp.int32, (ROWS, ROWS), 1)
                grads = grads - (row_ids == col_ids).astype(F32)
            grad_t[side, slot] = grads.astype(BF)

        def column(j, carry):
            cols = tile_at(j, TILE)
            part[slot, :, cols] = (
                dot_nn(grad_t[0, slot], score[0, :, cols]) + dot_nn(grad_t[1, slot], score[1, :, cols])
            ).astype(BF)
            return carry

        lax.fori_loop(0, WIDTH // TILE, column, 0)

    def tile_pair(hop):
        def one(i, carry):
            tile_grads(hop + i * (8 - 2 * hop), False)
            return carry

        lax.fori_loop(0, 2, one, 0)

    def score_grad(side, store, first, count):
        def column(j, carry):
            cols = tile_at(j, TILE)
            total = dot_tn(grad_t[side, 0], audio[0, :, cols])
            for slot in range(1, 8):
                total += dot_tn(grad_t[side, slot], audio[slot, :, cols])
            store(cols, total)
            return carry

        lax.fori_loop(first, first + count, column, 0)

    def unit_grad(tower, value_of, first, count):
        def step(rows):
            grad = factor * value_of(rows)
            vec = unit[tower, rows, :]
            radial = jnp.sum(vec * grad, axis=-1, keepdims=True)
            norm = length[tower, rows, 0:1]
            proj_grad[tower, rows, :] = ((grad - vec * radial) / norm).astype(BF)

        rows_in(first, count, step)

    def back(tower, weight, out):
        def column(j, carry):
            cols = tile_at(j, TILE)
            out[:, cols] = dot_nt(proj_grad[tower], weight[cols, :]).astype(BF)
            return carry

        lax.fori_loop(0, WIDTH // TILE, column, 0)

    def transpose(tower, side, feat):
        def step(z, carry):
            cols = tile_at(z, 128)
            feat_t[tower, side, cols, :] = feat[:, cols].T
            return carry

        lax.fori_loop(0, 8, step, 0)

    def feat_copy(tower, feat):
        return remote(feat, feat_other.at[tower], core_send.at[tower, 0], core_recv.at[tower, 0], device(dc=1))

    def proj_copy(tower):
        cols = pl.ds(pl.multiple_of(lax.rem(core + 1, 2) * 512, 512), 512)
        return remote(
            proj_grad.at[tower, :, cols], proj_other.at[tower],
            core_send.at[tower, 1], core_recv.at[tower, 1], device(dc=1),
        )

    def weight_part(tower, order):
        pair = lax.rem(yy // 2 + 1 + order, 2)
        own_cols = tile_at(core * 2 + pair, 256)
        other_cols = tile_at(pair, 256)

        def step(i, carry):
            rows = tile_at(i, 512)
            value = dot_nn(feat_t[tower, 0, rows, :], proj_grad[tower, :, own_cols])
            value += dot_nn(feat_t[tower, 1, rows, :], proj_other[tower, :, other_cols])
            value = value.astype(BF)
            for z in range(4):
                for q in range(2):
                    for x in range(4):
                        for route in range(2):
                            first = z * 128 + x * 32 + route * 16
                            half[tower, pair * 2 + q, route, x, i * 4 + z] = value[
                                first : first + 16, q * 128 : q * 128 + 128
                            ]
            return carry

        lax.fori_loop(0, 2, step, 0)

    def y_copy(tower, k):
        return remote(
            half.at[tower, lax.rem(yy + k, 4), 0], y_in.at[tower, k - 1],
            one_send.at[tower, 0], one_recv.at[tower, 0], device(dy=k),
        )

    def x_copy(tower, k):
        return remote(
            half.at[tower, :, 1, lax.rem(xx + k, 4)], x_in.at[tower, k - 1],
            one_send.at[tower, 1], one_recv.at[tower, 1], device(dx=k),
        )

    def launch_some(tower, order):
        if order == 0:
            launch(y_copy(tower, 2))
            launch(y_copy(tower, 3 - 2 * lax.rem(yy, 2)))
        else:
            for k in (2, 1, 3):
                launch(x_copy(tower, k))
            launch(y_copy(tower, 1 + 2 * lax.rem(yy, 2)))

    def two_copies(tower):
        copies = []
        for k in (2, 1, 3):
            copies.append(remote(
                y_sum.at[tower, lax.rem(xx + k, 4)], x_in2.at[tower, k - 1],
                two_send.at[tower, 0], two_recv.at[tower, 0], device(dx=k),
            ))
            copies.append(remote(
                x_sum.at[tower, lax.rem(yy + k, 4)], y_in2.at[tower, k - 1],
                two_send.at[tower, 1], two_recv.at[tower, 1], device(dy=k),
            ))
        return copies

    def z_copies(tower):
        return [
            remote(
                z_out.at[tower, lax.rem(zz + k, 8)], z_in.at[tower, k - 1],
                z_send.at[tower, 0], z_recv.at[tower, 0], device(dz=k),
            )
            for k in (4, 3, 5, 2, 6, 1, 7)
        ]

    place = (core * 4 + yy) * 2 + xl

    def all_copies(tower):
        return [
            remote(
                done.at[tower, place], done.at[tower, place],
                all_send.at[tower, 0], all_recv.at[tower, 0], flat_dp(k),
            )
            for k in range(1, 16)
        ]

    def stage_waits(tower, name):
        bufs, send, recv = {
            "one": ((y_in, x_in), one_send, one_recv),
            "two": ((x_in2, y_in2), two_send, two_recv),
            "z": ((z_in,), z_send, z_recv),
            "all": ((done,), all_send, all_recv),
        }[name]
        copies = []
        for i, buf in enumerate(bufs):
            view = buf.at[tower, pl.ds(0, 15)] if name == "all" else buf.at[tower]
            copies.append(remote(view, view, send.at[tower, i], recv.at[tower, i], device(dc=1)))
        return copies

    def stage_one_sum(tower):
        for copy in stage_waits(tower, "one"):
            copy.wait_recv()

        def step(i, carry):
            total = half[tower, yy, 0, i].astype(F32)
            for k in range(3):
                total += y_in[tower, k, i].astype(F32)
            y_sum[tower, i] = total.astype(BF)
            total = half[tower, i, 1, xx].astype(F32)
            for k in range(3):
                total += x_in[tower, k, i].astype(F32)
            x_sum[tower, i] = total.astype(BF)
            return carry

        lax.fori_loop(0, 4, step, 0)
        launch_all(two_copies(tower))

    def stage_two_sum(tower):
        for copy in stage_waits(tower, "two"):
            copy.wait_recv()
        total = y_sum[tower, xx].astype(F32)
        for k in range(3):
            total += x_in2[tower, k].astype(F32)
        z_out[tower, :, 0] = total.astype(BF)
        total = x_sum[tower, yy].astype(F32)
        for k in range(3):
            total += y_in2[tower, k].astype(F32)
        z_out[tower, :, 1] = total.astype(BF)
        launch_all(z_copies(tower))

    def stage_z_sum(tower):
        for copy in stage_waits(tower, "z"):
            copy.wait_recv()
        total = z_out[tower, zz].astype(F32)
        for k in range(7):
            total += z_in[tower, k].astype(F32)
        done[tower, place] = total.astype(BF)
        launch_all(all_copies(tower))

    def stage_all(tower, out):
        for copy in stage_waits(tower, "all"):
            copy.wait_recv()
        for q in range(8):
            for half_rows in range(2):
                for route in range(2):
                    first = half_rows * 32 + route * 16
                    out[first : first + 16, q * 128 : q * 128 + 128] = done[tower, q * 2 + half_rows, route].astype(F32)

    loads[0].wait()
    loads[1].wait()
    project(1, feat_a, weight_a, store_audio)
    pl.semaphore_wait(barrier, len(peers))
    for chunk in CHUNKS:
        for way in (PLUS, MINUS):
            launch(gather_copy(way, 1, chunk))
    loads[2].wait()
    loads[3].wait()
    project(0, feat_s, weight_s, store_score)
    pair = remote(score.at[0], score.at[1], side_send.at[0], side_recv.at[0], device(dx=2))
    launch(pair)
    launch(feat_copy(0, feat_s))
    launch(feat_copy(1, feat_a))
    transpose(0, 0, feat_s)
    transpose(1, 0, feat_a)

    for hop in range(1, 5):
        for chunk in CHUNKS:
            for way in (PLUS, MINUS):
                if hop == 4 and chunk not in GATHER_FAR[way]:
                    continue
                gather_copy(way, hop, chunk).wait_recv()
                if hop < 3 or (hop == 3 and chunk in GATHER_FAR[way]):
                    launch(gather_copy(way, hop + 1, chunk))
        if hop == 1:
            pair.wait_recv()
            tile_grads(0, True)
            for tower, feat in enumerate((feat_s, feat_a)):
                feat_copy(tower, feat).wait_recv()
                transpose(tower, 1, feat_other.at[tower])
        if hop < 4:
            tile_pair(hop)
        else:
            tile_grads(4, False)
        if hop >= 3:
            for way in (PLUS, MINUS):
                for chunk in SUM_FAR[way] if hop == 4 else SUM_FAR[1 - way]:
                    launch(ring_copy(way, 4 - hop, chunk))

    def store_side(cols, value):
        side_out[:, cols] = value.astype(BF)

    def store_own(cols, value):
        emb_grad[:, cols] = value

    side = remote(side_out, side_in, side_send.at[1], side_recv.at[1], device(dx=2))
    def own_column(j):
        return lambda: score_grad(0, store_own, j, 1)

    def score_unit():
        side.wait_recv()
        unit_grad(0, lambda rows: emb_grad[rows, :] + side_in[rows, :].astype(F32), 0, ROWS)
        launch(proj_copy(0))

    def score_first():
        proj_copy(0).wait_recv()
        weight_part(0, 0)

    def score_second():
        weight_part(0, 1)
        launch_some(0, 0)
        launch_some(0, 1)

    def score_back():
        back(0, weight_s, back_s)

    beside = {
        0: own_column(0), 1: own_column(1), 2: own_column(2), 3: own_column(3),
        6: score_unit, 7: score_first, 8: score_second, 9: score_back,
        11: lambda: stage_one_sum(0),
    }
    takes = []
    for hop, table in ((1, 1), (0, 0), (2, 1), (1, 0), (3, 1), (2, 0)):
        for k in range(2):
            takes.append([(way, hop, SUM_FAR[way ^ table][k]) for way in (PLUS, MINUS)])

    score_grad(1, store_side, 0, 4)
    launch(side)
    for i, both in enumerate(takes):
        for way, hop, chunk in both:
            ring_take(way, hop, chunk)
        if i in beside:
            beside[i]()

    def audio_value(rows):
        return (
            part[0, rows, :].astype(F32) + ring[PLUS, 3, rows, :].astype(F32) + ring[MINUS, 3, rows, :].astype(F32)
        )

    for k in range(2):
        for way in (PLUS, MINUS):
            ring_take(way, 3, SUM_FAR[way][k])
            unit_grad(1, audio_value, *SUM_FAR[way][k])
    launch(proj_copy(1))
    stage_two_sum(0)
    proj_copy(1).wait_recv()
    weight_part(1, 0)
    launch_some(1, 0)
    weight_part(1, 1)
    launch_some(1, 1)
    back(1, weight_a, back_a)
    stage_one_sum(1)
    stage_z_sum(0)
    stage_two_sum(1)
    stage_all(0, rows_s)
    stage_z_sum(1)
    stage_all(1, rows_a)

    for way in (PLUS, MINUS):
        for hop in range(4):
            for kind in range(2):
                far_rows = (GATHER_FAR, SUM_FAR)[kind][way]
                edge = hop == (3, 0)[kind]
                rows = pl.ds(far_rows[0][0], far_rows[0][1] + far_rows[1][1]) if edge else pl.ds(0, ROWS)
                buf = (audio.at[1, rows], ring.at[way, 1, rows])[kind]
                sem = (gather_send, ring_send)[kind].at[way, hop]
                remote(buf, buf, sem, (gather_recv, ring_recv)[kind].at[way, hop, 0], device(dz=1)).wait_send()
    pair.wait_send()
    side.wait_send()
    for tower in range(2):
        feat_copy(tower, (feat_s, feat_a)[tower]).wait_send()
        proj_copy(tower).wait_send()
        for name in ("one", "two", "z", "all"):
            for copy in stage_waits(tower, name):
                copy.wait_send()


def finish(*refs):
    copies = [pltpu.make_async_copy(refs[i], refs[4 + i], refs[8].at[i]) for i in range(4)]
    for copy in copies:
        copy.start()
    for copy in copies:
        copy.wait()


def body(score_feats, audio_feats, score_weight, audio_weight, log_temp, logit_bias, loss_scale):
    groups_rows = float(lax.axis_size("dp") * lax.axis_size("blk") * score_feats.shape[1])
    anywhere = pl.BlockSpec(memory_space=pl.ANY)
    rows = jax.ShapeDtypeStruct((ROWS, WIDTH), BF)
    sums = jax.ShapeDtypeStruct((64, WIDTH), F32)
    dma = pltpu.SemaphoreType.DMA
    scratch = [
        pltpu.VMEM((ROWS, WIDTH), BF),
        pltpu.VMEM((ROWS, WIDTH), BF),
        pltpu.VMEM((WIDTH, WIDTH), BF),
        pltpu.VMEM((WIDTH, WIDTH), BF),
        pltpu.SMEM((1,), F32),
        pltpu.SMEM((1,), F32),
        pltpu.SMEM((1,), F32),
        pltpu.VMEM((2, 2, WIDTH, ROWS), BF),
        dma((7,)),
        pltpu.VMEM((2, ROWS, WIDTH), F32),
        pltpu.VMEM((2, ROWS, 128), F32),
        pltpu.VMEM((8, ROWS, WIDTH), BF),
        pltpu.VMEM((2, ROWS, WIDTH), BF),
        pltpu.VMEM((2, 8, ROWS, ROWS), BF),
        pltpu.VMEM((8, ROWS, WIDTH), BF),
        pltpu.VMEM((2, 4, ROWS, WIDTH), BF),
        pltpu.VMEM((ROWS, WIDTH), BF),
        pltpu.VMEM((ROWS, WIDTH), BF),
        pltpu.VMEM((ROWS, WIDTH), F32),
        pltpu.VMEM((2, ROWS, WIDTH), BF),
        pltpu.VMEM((2, ROWS, WIDTH), BF),
        pltpu.VMEM((2, ROWS, WIDTH // 2), BF),
        pltpu.VMEM((2, 4, 2, 4, 8, 16, 128), BF),
        pltpu.VMEM((2, 3, 4, 8, 16, 128), BF),
        pltpu.VMEM((2, 3, 4, 8, 16, 128), BF),
        pltpu.VMEM((2, 4, 8, 16, 128), BF),
        pltpu.VMEM((2, 4, 8, 16, 128), BF),
        pltpu.VMEM((2, 3, 8, 16, 128), BF),
        pltpu.VMEM((2, 3, 8, 16, 128), BF),
        pltpu.VMEM((2, 8, 2, 16, 128), BF),
        pltpu.VMEM((2, 7, 2, 16, 128), BF),
        pltpu.VMEM((2, 16, 2, 16, 128), BF),
        dma((2, 4)),
        dma((2, 4, 4)),
        dma((2, 4)),
        dma((2, 4, 4)),
        dma((2,)),
        dma((2,)),
        dma((2, 2)),
        dma((2, 2)),
        dma((2, 2)),
        dma((2, 2)),
        dma((2, 2)),
        dma((2, 2)),
        dma((2, 1)),
        dma((2, 1)),
        dma((2, 1)),
        dma((2, 1)),
    ]
    shapes = (rows, rows, sums, sums)
    vmem = pl.BlockSpec(memory_space=pltpu.VMEM)
    results = pl.pallas_call(
        functools.partial(kernel, groups_rows),
        out_shape=tuple(pltpu.VMEM(v.shape, v.dtype) for v in shapes),
        in_specs=[anywhere] * 7,
        out_specs=(vmem,) * 4,
        scratch_shapes=scratch,
        compiler_params=pltpu.CompilerParams(
            collective_id=0, has_side_effects=True, vmem_limit_bytes=52 * 2**20
        ),
    )(*(
        pltpu.with_memory_space_constraint(v, pltpu.HBM)
        for v in (score_feats[0], audio_feats[0], score_weight, audio_weight)
    ), log_temp, logit_bias, loss_scale)
    back_s, back_a, rows_s, rows_a = pl.pallas_call(
        finish,
        out_shape=shapes,
        in_specs=[vmem] * 4,
        out_specs=(anywhere,) * 4,
        scratch_shapes=[dma((4,))],
    )(*(pltpu.with_memory_space_constraint(v, pltpu.VMEM) for v in results))
    return back_s[None], back_a[None], rows_s, rows_a


def solution(mesh):
    in_specs = (P("dp", "blk", None), P("dp", "blk", None), P(), P(), P(), P(), P())
    out_specs = (P("dp", "blk", None), P("dp", "blk", None), P("blk", None), P("blk", None))
    return jax.shard_map(body, mesh=mesh, in_specs=in_specs, out_specs=out_specs, check_vma=False)
```

```python
import functools

import jax
import jax.numpy as jnp
from jax import lax
from jax.experimental import pallas as pl
from jax.experimental.pallas import tpu as pltpu
from jax.sharding import PartitionSpec as P

MESH = pl.DeviceIdType.MESH
BF = jnp.bfloat16
F32 = jnp.float32
ROWS = 240
WIDTH = 1024
TILE = 256
STEP = 48

LOW = ((0, 64), (64, 48))
HIGH = ((112, 64), (176, 64))
CHUNKS = LOW + HIGH
PLUS, MINUS = 0, 1
GATHER_FAR = {PLUS: HIGH, MINUS: LOW}
SUM_FAR = {PLUS: LOW, MINUS: HIGH}


def dot_nn(a, b):
    return lax.dot_general(a, b, (((1,), (0,)), ((), ())), preferred_element_type=F32)


def dot_nt(a, b):
    return lax.dot_general(a, b, (((1,), (1,)), ((), ())), preferred_element_type=F32)


def dot_tn(a, b):
    return lax.dot_general(a, b, (((0,), (0,)), ((), ())), preferred_element_type=F32)


def tile_at(index, size):
    return pl.ds(pl.multiple_of(index * size, size), size)


def kernel(
    groups_rows,
    feat_s_in, feat_a_in, weight_s_in, weight_a_in, temp_ref, bias_ref, scale_ref,
    back_s, back_a, rows_s, rows_a,
    feat_s, feat_a, weight_s, weight_a, feat_t,
    load_sem,
    unit, length, audio, score, grad_t, part, ring, side_out, side_in, emb_grad, proj_grad,
    feat_other, proj_other, half, y_in, x_in, y_sum, x_sum, x_in2, y_in2, z_out, z_in, done,
    gather_send, gather_recv, ring_send, ring_recv, side_send, side_recv,
    core_send, core_recv, one_send, one_recv, two_send, two_recv, z_send, z_recv, all_send, all_recv,
):
    blk, dp = lax.axis_index("blk"), lax.axis_index("dp")
    zz, xh = blk // 2, lax.rem(blk, 2)
    xl, yy, core = dp // 8, lax.rem(dp // 2, 4), lax.rem(dp, 2)
    xx = xh * 2 + xl

    def device(dx=0, dy=0, dz=0, dc=0):
        x = lax.rem(xx + dx, 4)
        y = lax.rem(yy + dy, 4)
        z = lax.rem(zz + dz, 8)
        c = lax.rem(core + dc, 2)
        return {"blk": z * 2 + x // 2, "dp": (lax.rem(x, 2) * 4 + y) * 2 + c}

    def flat_dp(offset):
        return {"blk": blk, "dp": lax.rem(dp + offset, 16)}

    def remote(src, dst, send, recv, target):
        return pltpu.make_async_remote_copy(
            src_ref=src, dst_ref=dst, send_sem=send, recv_sem=recv, device_id=target, device_id_type=MESH
        )

    barrier = pltpu.get_barrier_semaphore()
    peers = [device(dz=1), device(dz=7), device(dc=1)]
    peers += [device(dx=k) for k in (2, 1, 3)] + [device(dy=k) for k in (2, 1, 3)]
    for peer in peers:
        pl.semaphore_signal(barrier, inc=1, device_id=peer, device_id_type=MESH)

    loads = [
        pltpu.make_async_copy(src, dst, load_sem.at[i])
        for i, (src, dst) in enumerate((
            (feat_a_in, feat_a), (weight_a_in, weight_a), (feat_s_in, feat_s), (weight_s_in, weight_s),
        ))
    ]
    for copy in loads:
        copy.start()

    temper = jnp.exp(jnp.full((1, 1), temp_ref[0], F32))
    bias = bias_ref[0]
    factor = scale_ref[0] * temper / groups_rows

    def launch(copy):
        copy.start()

    def launch_all(copies):
        for copy in copies:
            copy.start()

    def rows_in(first, count, fn):
        def step(i, carry):
            fn(pl.ds(pl.multiple_of(first + i * 16, 16), 16))
            return carry

        lax.fori_loop(0, count // 16, step, 0, unroll=True)

    def project(tower, feat, weight, store):
        def column(j, carry):
            cols = tile_at(j, TILE)
            unit[tower, :, cols] = dot_nn(feat[...], weight[:, cols])
            return carry

        lax.fori_loop(0, WIDTH // TILE, column, 0)

        def scale(i, carry):
            rows = tile_at(i, STEP)
            value = unit[tower, rows, :]
            norm = jnp.sqrt(jnp.sum(value * value, axis=-1, keepdims=True) + 1e-06)
            value = value / norm
            unit[tower, rows, :] = value
            length[tower, rows, :] = jnp.broadcast_to(norm, (STEP, 128))
            store(rows, value.astype(BF))
            return carry

        lax.fori_loop(0, ROWS // STEP, scale, 0)

    def store_audio(rows, value):
        audio[0, rows, :] = value

    def store_score(rows, value):
        score[0, rows, :] = value

    def gather_copy(way, hop, chunk):
        first, count = chunk
        rows = pl.ds(first, count)
        if way == PLUS:
            here, there = (8 - (hop - 1)) % 8, 8 - hop
        else:
            here, there = hop - 1, hop
        index = CHUNKS.index(chunk)
        return remote(
            audio.at[here, rows], audio.at[there, rows],
            gather_send.at[way, hop - 1], gather_recv.at[way, hop - 1, index],
            device(dz=1 if way == PLUS else 7),
        )

    def ring_slot(way, ahead):
        return ahead if way == PLUS else (8 - ahead) % 8

    def ring_copy(way, hop, chunk):
        first, count = chunk
        rows = pl.ds(first, count)
        start = 0 if chunk in SUM_FAR[way] else 1
        src = part.at[ring_slot(way, 4 - hop), rows] if hop == start else ring.at[way, hop - 1, rows]
        index = CHUNKS.index(chunk)
        return remote(
            src, ring.at[way, hop, rows],
            ring_send.at[way, hop], ring_recv.at[way, hop, index],
            device(dz=1 if way == PLUS else 7),
        )

    def ring_take(way, hop, chunk):
        ring_copy(way, hop, chunk).wait_recv()
        if hop < 3:
            slot = ring_slot(way, 3 - hop)

            def add(rows):
                ring[way, hop, rows, :] = (
                    ring[way, hop, rows, :].astype(F32) + part[slot, rows, :].astype(F32)
                ).astype(BF)

            rows_in(chunk[0], chunk[1], add)
            launch(ring_copy(way, hop + 1, chunk))

    def tile_grads(slot, own):
        for side in range(2):
            logits = temper * dot_nt(audio[slot], score[side]) + bias
            grads = jax.nn.sigmoid(logits)
            if own and side == 0:
                row_ids = lax.broadcasted_iota(jnp.int32, (ROWS, ROWS), 0)
                col_ids = lax.broadcasted_iota(jnp.int32, (ROWS, ROWS), 1)
                grads = grads - (row_ids == col_ids).astype(F32)
            grad_t[side, slot] = grads.astype(BF)

        def column(j, carry):
            cols = tile_at(j, TILE)
            part[slot, :, cols] = (
                dot_nn(grad_t[0, slot], score[0, :, cols]) + dot_nn(grad_t[1, slot], score[1, :, cols])
            ).astype(BF)
            return carry

        lax.fori_loop(0, WIDTH // TILE, column, 0)

    def tile_pair(hop):
        def one(i, carry):
            tile_grads(hop + i * (8 - 2 * hop), False)
            return carry

        lax.fori_loop(0, 2, one, 0)

    def score_grad(side, store, first, count):
        def column(j, carry):
            cols = tile_at(j, TILE)
            total = dot_tn(grad_t[side, 0], audio[0, :, cols])
            for slot in range(1, 8):
                total += dot_tn(grad_t[side, slot], audio[slot, :, cols])
            store(cols, total)
            return carry

        lax.fori_loop(first, first + count, column, 0)

    def unit_grad(tower, value_of, first, count):
        def step(rows):
            grad = factor * value_of(rows)
            vec = unit[tower, rows, :]
            radial = jnp.sum(vec * grad, axis=-1, keepdims=True)
            norm = length[tower, rows, 0:1]
            proj_grad[tower, rows, :] = ((grad - vec * radial) / norm).astype(BF)

        rows_in(first, count, step)

    def back(tower, weight, out):
        def column(j, carry):
            cols = tile_at(j, TILE)
            out[:, cols] = dot_nt(proj_grad[tower], weight[cols, :]).astype(BF)
            return carry

        lax.fori_loop(0, WIDTH // TILE, column, 0)

    def transpose(tower, side, feat):
        def step(z, carry):
            cols = tile_at(z, 128)
            feat_t[tower, side, cols, :] = feat[:, cols].T
            return carry

        lax.fori_loop(0, 8, step, 0)

    def feat_copy(tower, feat):
        return remote(feat, feat_other.at[tower], core_send.at[tower, 0], core_recv.at[tower, 0], device(dc=1))

    def proj_copy(tower, first=0, count=ROWS):
        cols = pl.ds(pl.multiple_of(lax.rem(core + 1, 2) * 512, 512), 512)
        return remote(
            proj_grad.at[tower, pl.ds(first, count), cols], proj_other.at[tower, pl.ds(first, count)],
            core_send.at[tower, 1], core_recv.at[tower, 1], device(dc=1),
        )

    def weight_part(tower, order):
        pair = lax.rem(yy // 2 + 1 + order, 2)
        own_cols = tile_at(core * 2 + pair, 256)
        other_cols = tile_at(pair, 256)

        def step(i, carry):
            rows = tile_at(i, 512)
            value = dot_nn(feat_t[tower, 0, rows, :], proj_grad[tower, :, own_cols])
            value += dot_nn(feat_t[tower, 1, rows, :], proj_other[tower, :, other_cols])
            value = value.astype(BF)
            for z in range(4):
                for q in range(2):
                    for x in range(4):
                        for route in range(2):
                            first = z * 128 + x * 32 + route * 16
                            half[tower, pair * 2 + q, route, x, i * 4 + z] = value[
                                first : first + 16, q * 128 : q * 128 + 128
                            ]
            return carry

        lax.fori_loop(0, 2, step, 0)

    def y_copy(tower, k):
        return remote(
            half.at[tower, lax.rem(yy + k, 4), 0], y_in.at[tower, k - 1],
            one_send.at[tower, 0], one_recv.at[tower, 0], device(dy=k),
        )

    def x_copy(tower, order, k):
        blocks = pl.ds(lax.rem(yy // 2 + 1 + order, 2) * 2, 2)
        return remote(
            half.at[tower, blocks, 1, lax.rem(xx + k, 4)], x_in.at[tower, k - 1, blocks],
            one_send.at[tower, 1], one_recv.at[tower, 1], device(dx=k),
        )

    def launch_some(tower, order):
        launch(x_copy(tower, order, 2))
        if order == 0:
            launch(y_copy(tower, 2))
            launch(y_copy(tower, 3 - 2 * lax.rem(yy, 2)))
        else:
            launch(y_copy(tower, 1 + 2 * lax.rem(yy, 2)))
        launch(x_copy(tower, order, 1))
        launch(x_copy(tower, order, 3))

    def two_copies(tower, route):
        if route == 0:
            return [
                remote(
                    y_sum.at[tower, lax.rem(xx + k, 4)], x_in2.at[tower, k - 1],
                    two_send.at[tower, 0], two_recv.at[tower, 0], device(dx=k),
                )
                for k in (2, 1, 3)
            ]
        return [
            remote(
                x_sum.at[tower, lax.rem(yy + k, 4)], y_in2.at[tower, k - 1],
                two_send.at[tower, 1], two_recv.at[tower, 1], device(dy=k),
            )
            for k in (2, 1, 3)
        ]

    def z_copies(tower):
        return [
            remote(
                z_out.at[tower, lax.rem(zz + k, 8)], z_in.at[tower, k - 1],
                z_send.at[tower, 0], z_recv.at[tower, 0], device(dz=k),
            )
            for k in (4, 3, 5, 2, 6, 1, 7)
        ]

    place = (core * 4 + yy) * 2 + xl

    def all_copies(tower):
        return [
            remote(
                done.at[tower, place], done.at[tower, place],
                all_send.at[tower, 0], all_recv.at[tower, 0], flat_dp(k),
            )
            for k in range(1, 16)
        ]

    def stage_waits(tower, name):
        bufs, send, recv = {
            "one": ((y_in, x_in), one_send, one_recv),
            "two": ((x_in2, y_in2), two_send, two_recv),
            "z": ((z_in,), z_send, z_recv),
            "all": ((done,), all_send, all_recv),
        }[name]
        copies = []
        for i, buf in enumerate(bufs):
            view = buf.at[tower, pl.ds(0, 15)] if name == "all" else buf.at[tower]
            copies.append(remote(view, view, send.at[tower, i], recv.at[tower, i], device(dc=1)))
        return copies

    def stage_one_sum(tower):
        first, second = stage_waits(tower, "one")
        first.wait_recv()

        def y_step(i, carry):
            total = half[tower, yy, 0, i].astype(F32)
            for k in range(3):
                total += y_in[tower, k, i].astype(F32)
            y_sum[tower, i] = total.astype(BF)
            return carry

        lax.fori_loop(0, 4, y_step, 0)
        launch_all(two_copies(tower, 0))
        second.wait_recv()

        def x_step(i, carry):
            total = half[tower, i, 1, xx].astype(F32)
            for k in range(3):
                total += x_in[tower, k, i].astype(F32)
            x_sum[tower, i] = total.astype(BF)
            return carry

        lax.fori_loop(0, 4, x_step, 0)
        launch_all(two_copies(tower, 1))

    def stage_two_sum(tower):
        for copy in stage_waits(tower, "two"):
            copy.wait_recv()
        total = y_sum[tower, xx].astype(F32)
        for k in range(3):
            total += x_in2[tower, k].astype(F32)
        z_out[tower, :, 0] = total.astype(BF)
        total = x_sum[tower, yy].astype(F32)
        for k in range(3):
            total += y_in2[tower, k].astype(F32)
        z_out[tower, :, 1] = total.astype(BF)
        launch_all(z_copies(tower))

    def stage_z_sum(tower):
        for copy in stage_waits(tower, "z"):
            copy.wait_recv()
        total = z_out[tower, zz].astype(F32)
        for k in range(7):
            total += z_in[tower, k].astype(F32)
        done[tower, place] = total.astype(BF)
        launch_all(all_copies(tower))

    def stage_all(tower, out):
        for copy in stage_waits(tower, "all"):
            copy.wait_recv()
        for q in range(8):
            for half_rows in range(2):
                for route in range(2):
                    first = half_rows * 32 + route * 16
                    out[first : first + 16, q * 128 : q * 128 + 128] = done[tower, q * 2 + half_rows, route].astype(F32)

    loads[0].wait()
    loads[1].wait()
    project(1, feat_a, weight_a, store_audio)
    pl.semaphore_wait(barrier, len(peers))
    for chunk in CHUNKS:
        for way in (PLUS, MINUS):
            launch(gather_copy(way, 1, chunk))
    loads[2].wait()
    loads[3].wait()
    project(0, feat_s, weight_s, store_score)
    pair = remote(score.at[0], score.at[1], side_send.at[0], side_recv.at[0], device(dx=2))
    launch(pair)
    launch(feat_copy(0, feat_s))
    launch(feat_copy(1, feat_a))
    transpose(0, 0, feat_s)
    transpose(1, 0, feat_a)

    for hop in range(1, 5):
        for chunk in CHUNKS:
            for way in (PLUS, MINUS):
                if hop == 4 and chunk not in GATHER_FAR[way]:
                    continue
                gather_copy(way, hop, chunk).wait_recv()
                if hop < 3 or (hop == 3 and chunk in GATHER_FAR[way]):
                    launch(gather_copy(way, hop + 1, chunk))
        if hop == 1:
            pair.wait_recv()
            tile_grads(0, True)
            for tower, feat in enumerate((feat_s, feat_a)):
                feat_copy(tower, feat).wait_recv()
                transpose(tower, 1, feat_other.at[tower])
        if hop < 4:
            tile_pair(hop)
        else:
            tile_grads(4, False)
        if hop >= 3:
            for way in (PLUS, MINUS):
                for chunk in SUM_FAR[way] if hop == 4 else SUM_FAR[1 - way]:
                    launch(ring_copy(way, 4 - hop, chunk))

    def store_side(cols, value):
        side_out[:, cols] = value.astype(BF)

    def store_own(cols, value):
        emb_grad[:, cols] = value

    side = remote(side_out, side_in, side_send.at[1], side_recv.at[1], device(dx=2))
    def own_column(j):
        return lambda: score_grad(0, store_own, j, 1)

    def score_unit():
        side.wait_recv()
        unit_grad(0, lambda rows: emb_grad[rows, :] + side_in[rows, :].astype(F32), 0, ROWS)
        launch(proj_copy(0))

    def score_first():
        proj_copy(0).wait_recv()
        weight_part(0, 0)

    def score_second():
        weight_part(0, 1)
        launch_some(0, 0)
        launch_some(0, 1)

    def score_back():
        back(0, weight_s, back_s)

    beside = {
        0: own_column(0), 1: own_column(1), 2: own_column(2), 3: own_column(3),
        6: score_unit, 7: score_first, 8: score_second, 9: score_back,
        11: lambda: stage_one_sum(0),
    }
    takes = []
    for hop, table in ((1, 1), (0, 0), (2, 1), (1, 0), (3, 1), (2, 0)):
        for k in range(2):
            takes.append([(way, hop, SUM_FAR[way ^ table][k]) for way in (PLUS, MINUS)])

    score_grad(1, store_side, 0, 4)
    launch(side)
    for i, both in enumerate(takes):
        for way, hop, chunk in both:
            ring_take(way, hop, chunk)
        if i in beside:
            beside[i]()

    def audio_value(rows):
        return (
            part[0, rows, :].astype(F32) + ring[PLUS, 3, rows, :].astype(F32) + ring[MINUS, 3, rows, :].astype(F32)
        )

    for k in range(2):
        for way in (PLUS, MINUS):
            ring_take(way, 3, SUM_FAR[way][k])
            unit_grad(1, audio_value, *SUM_FAR[way][k])
            launch(proj_copy(1, *SUM_FAR[way][k]))
    stage_two_sum(0)
    proj_copy(1).wait_recv()
    weight_part(1, 0)
    launch_some(1, 0)
    weight_part(1, 1)
    launch_some(1, 1)
    back(1, weight_a, back_a)
    stage_one_sum(1)
    stage_z_sum(0)
    stage_two_sum(1)
    stage_all(0, rows_s)
    stage_z_sum(1)
    stage_all(1, rows_a)

    for way in (PLUS, MINUS):
        for hop in range(4):
            for kind in range(2):
                far_rows = (GATHER_FAR, SUM_FAR)[kind][way]
                edge = hop == (3, 0)[kind]
                rows = pl.ds(far_rows[0][0], far_rows[0][1] + far_rows[1][1]) if edge else pl.ds(0, ROWS)
                buf = (audio.at[1, rows], ring.at[way, 1, rows])[kind]
                sem = (gather_send, ring_send)[kind].at[way, hop]
                remote(buf, buf, sem, (gather_recv, ring_recv)[kind].at[way, hop, 0], device(dz=1)).wait_send()
    pair.wait_send()
    side.wait_send()
    for tower in range(2):
        feat_copy(tower, (feat_s, feat_a)[tower]).wait_send()
        proj_copy(tower).wait_send()
        for name in ("one", "two", "z", "all"):
            for copy in stage_waits(tower, name):
                copy.wait_send()


def finish(*refs):
    copies = [pltpu.make_async_copy(refs[i], refs[4 + i], refs[8].at[i]) for i in range(4)]
    for copy in copies:
        copy.start()
    for copy in copies:
        copy.wait()


def body(score_feats, audio_feats, score_weight, audio_weight, log_temp, logit_bias, loss_scale):
    groups_rows = float(lax.axis_size("dp") * lax.axis_size("blk") * score_feats.shape[1])
    anywhere = pl.BlockSpec(memory_space=pl.ANY)
    smem = pl.BlockSpec(memory_space=pltpu.SMEM)
    rows = jax.ShapeDtypeStruct((ROWS, WIDTH), BF)
    sums = jax.ShapeDtypeStruct((64, WIDTH), F32)
    dma = pltpu.SemaphoreType.DMA
    scratch = [
        pltpu.VMEM((ROWS, WIDTH), BF),
        pltpu.VMEM((ROWS, WIDTH), BF),
        pltpu.VMEM((WIDTH, WIDTH), BF),
        pltpu.VMEM((WIDTH, WIDTH), BF),
        pltpu.VMEM((2, 2, WIDTH, ROWS), BF),
        dma((4,)),
        pltpu.VMEM((2, ROWS, WIDTH), F32),
        pltpu.VMEM((2, ROWS, 128), F32),
        pltpu.VMEM((8, ROWS, WIDTH), BF),
        pltpu.VMEM((2, ROWS, WIDTH), BF),
        pltpu.VMEM((2, 8, ROWS, ROWS), BF),
        pltpu.VMEM((8, ROWS, WIDTH), BF),
        pltpu.VMEM((2, 4, ROWS, WIDTH), BF),
        pltpu.VMEM((ROWS, WIDTH), BF),
        pltpu.VMEM((ROWS, WIDTH), BF),
        pltpu.VMEM((ROWS, WIDTH), F32),
        pltpu.VMEM((2, ROWS, WIDTH), BF),
        pltpu.VMEM((2, ROWS, WIDTH), BF),
        pltpu.VMEM((2, ROWS, WIDTH // 2), BF),
        pltpu.VMEM((2, 4, 2, 4, 8, 16, 128), BF),
        pltpu.VMEM((2, 3, 4, 8, 16, 128), BF),
        pltpu.VMEM((2, 3, 4, 8, 16, 128), BF),
        pltpu.VMEM((2, 4, 8, 16, 128), BF),
        pltpu.VMEM((2, 4, 8, 16, 128), BF),
        pltpu.VMEM((2, 3, 8, 16, 128), BF),
        pltpu.VMEM((2, 3, 8, 16, 128), BF),
        pltpu.VMEM((2, 8, 2, 16, 128), BF),
        pltpu.VMEM((2, 7, 2, 16, 128), BF),
        pltpu.VMEM((2, 16, 2, 16, 128), BF),
        dma((2, 4)),
        dma((2, 4, 4)),
        dma((2, 4)),
        dma((2, 4, 4)),
        dma((2,)),
        dma((2,)),
        dma((2, 2)),
        dma((2, 2)),
        dma((2, 2)),
        dma((2, 2)),
        dma((2, 2)),
        dma((2, 2)),
        dma((2, 1)),
        dma((2, 1)),
        dma((2, 1)),
        dma((2, 1)),
    ]
    shapes = (rows, rows, sums, sums)
    vmem = pl.BlockSpec(memory_space=pltpu.VMEM)
    results = pl.pallas_call(
        functools.partial(kernel, groups_rows),
        out_shape=tuple(pltpu.VMEM(v.shape, v.dtype) for v in shapes),
        in_specs=[anywhere] * 4 + [smem] * 3,
        out_specs=(vmem,) * 4,
        scratch_shapes=scratch,
        compiler_params=pltpu.CompilerParams(
            collective_id=0, has_side_effects=True, vmem_limit_bytes=52 * 2**20
        ),
    )(*(
        pltpu.with_memory_space_constraint(v, pltpu.HBM)
        for v in (score_feats[0], audio_feats[0], score_weight, audio_weight)
    ), log_temp, logit_bias, loss_scale)
    back_s, back_a, rows_s, rows_a = pl.pallas_call(
        finish,
        out_shape=shapes,
        in_specs=[vmem] * 4,
        out_specs=(anywhere,) * 4,
        scratch_shapes=[dma((4,))],
    )(*(pltpu.with_memory_space_constraint(v, pltpu.VMEM) for v in results))
    return back_s[None], back_a[None], rows_s, rows_a


def solution(mesh):
    in_specs = (P("dp", "blk", None), P("dp", "blk", None), P(), P(), P(), P(), P())
    out_specs = (P("dp", "blk", None), P("dp", "blk", None), P("blk", None), P("blk", None))
    return jax.shard_map(body, mesh=mesh, in_specs=in_specs, out_specs=out_specs, check_vma=False)
```

```python
import functools

import jax
import jax.numpy as jnp
from jax import lax
from jax.experimental import pallas as pl
from jax.experimental.pallas import tpu as pltpu
from jax.sharding import PartitionSpec as P

MESH = pl.DeviceIdType.MESH
BF = jnp.bfloat16
F32 = jnp.float32
ROWS = 240
WIDTH = 1024
TILE = 256
STEP = 48

LOW = ((0, 64), (64, 48))
HIGH = ((112, 64), (176, 64))
CHUNKS = LOW + HIGH
PLUS, MINUS = 0, 1
GATHER_FAR = {PLUS: HIGH, MINUS: LOW}
SUM_FAR = {PLUS: LOW, MINUS: HIGH}


def dot_nn(a, b):
    return lax.dot_general(a, b, (((1,), (0,)), ((), ())), preferred_element_type=F32)


def dot_nt(a, b):
    return lax.dot_general(a, b, (((1,), (1,)), ((), ())), preferred_element_type=F32)


def dot_tn(a, b):
    return lax.dot_general(a, b, (((0,), (0,)), ((), ())), preferred_element_type=F32)


def tile_at(index, size):
    return pl.ds(pl.multiple_of(index * size, size), size)


def kernel(
    groups_rows,
    feat_s_in, feat_a_in, weight_s_in, weight_a_in, temp_ref, bias_ref, scale_ref,
    back_s, back_a, rows_s, rows_a,
    feat_s, feat_a, weight_s, weight_a, feat_t,
    load_sem,
    unit, length, audio, score, grad_t, part, ring, side_out, side_in, emb_grad, proj_grad,
    feat_other, proj_other, half, y_in, x_in, y_sum, x_sum, x_in2, y_in2, z_out, z_in, done,
    gather_send, gather_recv, ring_send, ring_recv, side_send, side_recv,
    core_send, core_recv, one_send, one_recv, two_send, two_recv, z_send, z_recv, all_send, all_recv,
):
    blk, dp = lax.axis_index("blk"), lax.axis_index("dp")
    zz, xh = blk // 2, lax.rem(blk, 2)
    xl, yy, core = dp // 8, lax.rem(dp // 2, 4), lax.rem(dp, 2)
    xx = xh * 2 + xl

    def device(dx=0, dy=0, dz=0, dc=0):
        x = lax.rem(xx + dx, 4)
        y = lax.rem(yy + dy, 4)
        z = lax.rem(zz + dz, 8)
        c = lax.rem(core + dc, 2)
        return {"blk": z * 2 + x // 2, "dp": (lax.rem(x, 2) * 4 + y) * 2 + c}

    def flat_dp(offset):
        return {"blk": blk, "dp": lax.rem(dp + offset, 16)}

    def remote(src, dst, send, recv, target):
        return pltpu.make_async_remote_copy(
            src_ref=src, dst_ref=dst, send_sem=send, recv_sem=recv, device_id=target, device_id_type=MESH
        )

    barrier = pltpu.get_barrier_semaphore()
    peers = [device(dz=1), device(dz=7), device(dc=1)]
    peers += [device(dx=k) for k in (2, 1, 3)] + [device(dy=k) for k in (2, 1, 3)]
    for peer in peers:
        pl.semaphore_signal(barrier, inc=1, device_id=peer, device_id_type=MESH)

    loads = [
        pltpu.make_async_copy(src, dst, load_sem.at[i])
        for i, (src, dst) in enumerate((
            (feat_a_in, feat_a), (weight_a_in, weight_a), (feat_s_in, feat_s), (weight_s_in, weight_s),
        ))
    ]
    for copy in loads:
        copy.start()

    temper = jnp.exp(jnp.full((1, 1), temp_ref[0], F32))
    bias = bias_ref[0]
    factor = scale_ref[0] * temper / groups_rows

    def launch(copy):
        copy.start()

    def launch_all(copies):
        for copy in copies:
            copy.start()

    def rows_in(first, count, fn):
        def step(i, carry):
            fn(pl.ds(pl.multiple_of(first + i * 16, 16), 16))
            return carry

        lax.fori_loop(0, count // 16, step, 0, unroll=True)

    def project(tower, feat, weight, store):
        def column(j, carry):
            cols = tile_at(j, TILE)
            unit[tower, :, cols] = dot_nn(feat[...], weight[:, cols])
            return carry

        lax.fori_loop(0, WIDTH // TILE, column, 0)

        def scale(i, carry):
            rows = tile_at(i, STEP)
            value = unit[tower, rows, :]
            norm = jnp.sqrt(jnp.sum(value * value, axis=-1, keepdims=True) + 1e-06)
            value = value / norm
            unit[tower, rows, :] = value
            length[tower, rows, :] = jnp.broadcast_to(norm, (STEP, 128))
            store(rows, value.astype(BF))
            return carry

        lax.fori_loop(0, ROWS // STEP, scale, 0)

    def store_audio(rows, value):
        audio[0, rows, :] = value

    def store_score(rows, value):
        score[0, rows, :] = value

    def gather_copy(way, hop, chunk):
        first, count = chunk
        rows = pl.ds(first, count)
        if way == PLUS:
            here, there = (8 - (hop - 1)) % 8, 8 - hop
        else:
            here, there = hop - 1, hop
        index = CHUNKS.index(chunk)
        return remote(
            audio.at[here, rows], audio.at[there, rows],
            gather_send.at[way, hop - 1], gather_recv.at[way, hop - 1, index],
            device(dz=1 if way == PLUS else 7),
        )

    def ring_slot(way, ahead):
        return ahead if way == PLUS else (8 - ahead) % 8

    def ring_copy(way, hop, chunk):
        first, count = chunk
        rows = pl.ds(first, count)
        start = 0 if chunk in SUM_FAR[way] else 1
        src = part.at[ring_slot(way, 4 - hop), rows] if hop == start else ring.at[way, hop - 1, rows]
        index = CHUNKS.index(chunk)
        return remote(
            src, ring.at[way, hop, rows],
            ring_send.at[way, hop], ring_recv.at[way, hop, index],
            device(dz=1 if way == PLUS else 7),
        )

    def ring_take(way, hop, chunk):
        ring_copy(way, hop, chunk).wait_recv()
        if hop < 3:
            slot = ring_slot(way, 3 - hop)

            def add(rows):
                ring[way, hop, rows, :] = (
                    ring[way, hop, rows, :].astype(F32) + part[slot, rows, :].astype(F32)
                ).astype(BF)

            rows_in(chunk[0], chunk[1], add)
            launch(ring_copy(way, hop + 1, chunk))

    def tile_grads(slot, own):
        for side in range(2):
            logits = temper * dot_nt(audio[slot], score[side]) + bias
            grads = jax.nn.sigmoid(logits)
            if own and side == 0:
                row_ids = lax.broadcasted_iota(jnp.int32, (ROWS, ROWS), 0)
                col_ids = lax.broadcasted_iota(jnp.int32, (ROWS, ROWS), 1)
                grads = grads - (row_ids == col_ids).astype(F32)
            grad_t[side, slot] = grads.astype(BF)

        def column(j, carry):
            cols = tile_at(j, TILE)
            part[slot, :, cols] = (
                dot_nn(grad_t[0, slot], score[0, :, cols]) + dot_nn(grad_t[1, slot], score[1, :, cols])
            ).astype(BF)
            return carry

        lax.fori_loop(0, WIDTH // TILE, column, 0)

    def tile_pair(hop):
        def one(i, carry):
            tile_grads(hop + i * (8 - 2 * hop), False)
            return carry

        lax.fori_loop(0, 2, one, 0)

    def score_grad(side, store, first, count):
        def column(j, carry):
            cols = tile_at(j, TILE)
            total = dot_tn(grad_t[side, 0], audio[0, :, cols])
            for slot in range(1, 8):
                total += dot_tn(grad_t[side, slot], audio[slot, :, cols])
            store(cols, total)
            return carry

        lax.fori_loop(first, first + count, column, 0)

    def unit_grad(tower, value_of, first, count):
        def step(rows):
            grad = factor * value_of(rows)
            vec = unit[tower, rows, :]
            radial = jnp.sum(vec * grad, axis=-1, keepdims=True)
            norm = length[tower, rows, 0:1]
            proj_grad[tower, rows, :] = ((grad - vec * radial) / norm).astype(BF)

        rows_in(first, count, step)

    def back(tower, weight, out):
        def column(j, carry):
            cols = tile_at(j, TILE)
            out[:, cols] = dot_nt(proj_grad[tower], weight[cols, :]).astype(BF)
            return carry

        lax.fori_loop(0, WIDTH // TILE, column, 0)

    def transpose(tower, side, feat):
        def step(z, carry):
            cols = tile_at(z, 128)
            feat_t[tower, side, cols, :] = feat[:, cols].T
            return carry

        lax.fori_loop(0, 8, step, 0)

    def feat_copy(tower, feat):
        return remote(feat, feat_other.at[tower], core_send.at[tower, 0], core_recv.at[tower, 0], device(dc=1))

    def proj_copy(tower, first=0, count=ROWS):
        cols = pl.ds(pl.multiple_of(lax.rem(core + 1, 2) * 512, 512), 512)
        return remote(
            proj_grad.at[tower, pl.ds(first, count), cols], proj_other.at[tower, pl.ds(first, count)],
            core_send.at[tower, 1], core_recv.at[tower, 1], device(dc=1),
        )

    def weight_part(tower, order):
        pair = lax.rem(yy // 2 + 1 + order, 2)
        own_cols = tile_at(core * 2 + pair, 256)
        other_cols = tile_at(pair, 256)

        def step(i, carry):
            rows = tile_at(i, 512)
            value = dot_nn(feat_t[tower, 0, rows, :], proj_grad[tower, :, own_cols])
            value += dot_nn(feat_t[tower, 1, rows, :], proj_other[tower, :, other_cols])
            value = value.astype(BF)
            for z in range(4):
                for q in range(2):
                    for x in range(4):
                        for route in range(2):
                            first = z * 128 + x * 32 + route * 16
                            half[tower, pair * 2 + q, route, x, i * 4 + z] = value[
                                first : first + 16, q * 128 : q * 128 + 128
                            ]
            return carry

        lax.fori_loop(0, 2, step, 0)

    def y_copy(tower, k):
        return remote(
            half.at[tower, lax.rem(yy + k, 4), 0], y_in.at[tower, k - 1],
            one_send.at[tower, 0], one_recv.at[tower, 0], device(dy=k),
        )

    def x_copy(tower, order, k):
        blocks = pl.ds(lax.rem(yy // 2 + 1 + order, 2) * 2, 2)
        return remote(
            half.at[tower, blocks, 1, lax.rem(xx + k, 4)], x_in.at[tower, k - 1, blocks],
            one_send.at[tower, 1], one_recv.at[tower, 1], device(dx=k),
        )

    def launch_some(tower, order):
        launch(x_copy(tower, order, 2))
        if order == 0:
            launch(y_copy(tower, 2))
            launch(y_copy(tower, 3 - 2 * lax.rem(yy, 2)))
        else:
            launch(y_copy(tower, 1 + 2 * lax.rem(yy, 2)))
        launch(x_copy(tower, order, 1))
        launch(x_copy(tower, order, 3))

    def two_copies(tower, route):
        if route == 0:
            return [
                remote(
                    y_sum.at[tower, lax.rem(xx + k, 4)], x_in2.at[tower, k - 1],
                    two_send.at[tower, 0], two_recv.at[tower, 0], device(dx=k),
                )
                for k in (2, 1, 3)
            ]
        return [
            remote(
                x_sum.at[tower, lax.rem(yy + k, 4)], y_in2.at[tower, k - 1],
                two_send.at[tower, 1], two_recv.at[tower, 1], device(dy=k),
            )
            for k in (2, 1, 3)
        ]

    def z_copies(tower):
        return [
            remote(
                z_out.at[tower, lax.rem(zz + k, 8)], z_in.at[tower, k - 1],
                z_send.at[tower, 0], z_recv.at[tower, 0], device(dz=k),
            )
            for k in (4, 3, 5, 2, 6, 1, 7)
        ]

    place = (core * 4 + yy) * 2 + xl

    def all_copies(tower):
        return [
            remote(
                done.at[tower, place], done.at[tower, place],
                all_send.at[tower, 0], all_recv.at[tower, 0], flat_dp(k),
            )
            for k in range(1, 16)
        ]

    def stage_waits(tower, name):
        bufs, send, recv = {
            "one": ((y_in, x_in), one_send, one_recv),
            "two": ((x_in2, y_in2), two_send, two_recv),
            "z": ((z_in,), z_send, z_recv),
            "all": ((done,), all_send, all_recv),
        }[name]
        copies = []
        for i, buf in enumerate(bufs):
            view = buf.at[tower, pl.ds(0, 15)] if name == "all" else buf.at[tower]
            copies.append(remote(view, view, send.at[tower, i], recv.at[tower, i], device(dc=1)))
        return copies

    def stage_one_sum(tower):
        first, second = stage_waits(tower, "one")
        first.wait_recv()

        def y_step(i, carry):
            total = half[tower, yy, 0, i].astype(F32)
            for k in range(3):
                total += y_in[tower, k, i].astype(F32)
            y_sum[tower, i] = total.astype(BF)
            return carry

        lax.fori_loop(0, 4, y_step, 0)
        launch_all(two_copies(tower, 0))
        second.wait_recv()

        def x_step(i, carry):
            total = half[tower, i, 1, xx].astype(F32)
            for k in range(3):
                total += x_in[tower, k, i].astype(F32)
            x_sum[tower, i] = total.astype(BF)
            return carry

        lax.fori_loop(0, 4, x_step, 0)
        launch_all(two_copies(tower, 1))

    def stage_two_sum(tower):
        for copy in stage_waits(tower, "two"):
            copy.wait_recv()
        total = y_sum[tower, xx].astype(F32)
        for k in range(3):
            total += x_in2[tower, k].astype(F32)
        z_out[tower, :, 0] = total.astype(BF)
        total = x_sum[tower, yy].astype(F32)
        for k in range(3):
            total += y_in2[tower, k].astype(F32)
        z_out[tower, :, 1] = total.astype(BF)
        launch_all(z_copies(tower))

    def stage_z_sum(tower):
        for copy in stage_waits(tower, "z"):
            copy.wait_recv()
        total = z_out[tower, zz].astype(F32)
        for k in range(7):
            total += z_in[tower, k].astype(F32)
        done[tower, place] = total.astype(BF)
        launch_all(all_copies(tower))

    def stage_all(tower, out):
        for copy in stage_waits(tower, "all"):
            copy.wait_recv()
        for q in range(8):
            for half_rows in range(2):
                for route in range(2):
                    first = half_rows * 32 + route * 16
                    out[first : first + 16, q * 128 : q * 128 + 128] = done[tower, q * 2 + half_rows, route].astype(F32)

    loads[0].wait()
    loads[1].wait()
    project(1, feat_a, weight_a, store_audio)
    pl.semaphore_wait(barrier, len(peers))
    for chunk in CHUNKS:
        for way in (PLUS, MINUS):
            launch(gather_copy(way, 1, chunk))
    loads[2].wait()
    loads[3].wait()
    project(0, feat_s, weight_s, store_score)
    pair = remote(score.at[0], score.at[1], side_send.at[0], side_recv.at[0], device(dx=2))
    launch(pair)
    launch(feat_copy(0, feat_s))
    launch(feat_copy(1, feat_a))
    transpose(0, 0, feat_s)
    transpose(1, 0, feat_a)

    for hop in range(1, 5):
        for chunk in CHUNKS:
            for way in (PLUS, MINUS):
                if hop == 4 and chunk not in GATHER_FAR[way]:
                    continue
                gather_copy(way, hop, chunk).wait_recv()
                if hop < 3 or (hop == 3 and chunk in GATHER_FAR[way]):
                    launch(gather_copy(way, hop + 1, chunk))
        if hop == 1:
            pair.wait_recv()
            tile_grads(0, True)
            for tower, feat in enumerate((feat_s, feat_a)):
                feat_copy(tower, feat).wait_recv()
                transpose(tower, 1, feat_other.at[tower])
        if hop < 4:
            tile_pair(hop)
        else:
            tile_grads(4, False)
        if hop >= 3:
            for way in (PLUS, MINUS):
                for chunk in SUM_FAR[way] if hop == 4 else SUM_FAR[1 - way]:
                    launch(ring_copy(way, 4 - hop, chunk))

    def store_side(cols, value):
        side_out[:, cols] = value.astype(BF)

    def store_own(cols, value):
        emb_grad[:, cols] = value

    side = remote(side_out, side_in, side_send.at[1], side_recv.at[1], device(dx=2))
    def own_column(j):
        return lambda: score_grad(0, store_own, j, 1)

    def score_unit():
        side.wait_recv()
        unit_grad(0, lambda rows: emb_grad[rows, :] + side_in[rows, :].astype(F32), 0, ROWS)
        launch(proj_copy(0))

    def score_first():
        proj_copy(0).wait_recv()
        weight_part(0, 0)

    def score_second():
        weight_part(0, 1)
        launch_some(0, 0)
        launch_some(0, 1)

    def score_back():
        back(0, weight_s, back_s)

    beside = {
        0: own_column(0), 1: own_column(1), 2: own_column(2), 3: own_column(3),
        6: score_unit, 7: score_first, 8: score_second, 9: score_back,
        11: lambda: stage_one_sum(0),
    }
    takes = []
    for hop, table, k in (
        (1, 1, 0), (1, 1, 1), (0, 0, 0), (0, 0, 1), (2, 1, 0), (1, 0, 0),
        (1, 0, 1), (2, 1, 1), (3, 1, 0), (2, 0, 0), (2, 0, 1), (3, 1, 1),
    ):
        takes.append([(way, hop, SUM_FAR[way ^ table][k]) for way in (PLUS, MINUS)])

    score_grad(1, store_side, 0, 4)
    launch(side)
    for i, both in enumerate(takes):
        for way, hop, chunk in both:
            ring_take(way, hop, chunk)
        if i in beside:
            beside[i]()

    def audio_value(rows):
        return (
            part[0, rows, :].astype(F32) + ring[PLUS, 3, rows, :].astype(F32) + ring[MINUS, 3, rows, :].astype(F32)
        )

    for k in range(2):
        for way in (PLUS, MINUS):
            ring_take(way, 3, SUM_FAR[way][k])
            unit_grad(1, audio_value, *SUM_FAR[way][k])
            launch(proj_copy(1, *SUM_FAR[way][k]))
    stage_two_sum(0)
    proj_copy(1).wait_recv()
    weight_part(1, 0)
    launch_some(1, 0)
    weight_part(1, 1)
    launch_some(1, 1)
    back(1, weight_a, back_a)
    stage_one_sum(1)
    stage_z_sum(0)
    stage_two_sum(1)
    stage_all(0, rows_s)
    stage_z_sum(1)

    for way in (PLUS, MINUS):
        for hop in range(4):
            for kind in range(2):
                far_rows = (GATHER_FAR, SUM_FAR)[kind][way]
                edge = hop == (3, 0)[kind]
                rows = pl.ds(far_rows[0][0], far_rows[0][1] + far_rows[1][1]) if edge else pl.ds(0, ROWS)
                buf = (audio.at[1, rows], ring.at[way, 1, rows])[kind]
                sem = (gather_send, ring_send)[kind].at[way, hop]
                remote(buf, buf, sem, (gather_recv, ring_recv)[kind].at[way, hop, 0], device(dz=1)).wait_send()
    pair.wait_send()
    side.wait_send()
    for tower in range(2):
        feat_copy(tower, (feat_s, feat_a)[tower]).wait_send()
        proj_copy(tower).wait_send()
        for name in ("one", "two", "z", "all")[: 4 - tower]:
            for copy in stage_waits(tower, name):
                copy.wait_send()
    stage_all(1, rows_a)
    for copy in stage_waits(1, "all"):
        copy.wait_send()


def finish(*refs):
    copies = [pltpu.make_async_copy(refs[i], refs[4 + i], refs[8].at[i]) for i in range(4)]
    for copy in copies:
        copy.start()
    for copy in copies:
        copy.wait()


def body(score_feats, audio_feats, score_weight, audio_weight, log_temp, logit_bias, loss_scale):
    groups_rows = float(lax.axis_size("dp") * lax.axis_size("blk") * score_feats.shape[1])
    anywhere = pl.BlockSpec(memory_space=pl.ANY)
    smem = pl.BlockSpec(memory_space=pltpu.SMEM)
    rows = jax.ShapeDtypeStruct((ROWS, WIDTH), BF)
    sums = jax.ShapeDtypeStruct((64, WIDTH), F32)
    dma = pltpu.SemaphoreType.DMA
    scratch = [
        pltpu.VMEM((ROWS, WIDTH), BF),
        pltpu.VMEM((ROWS, WIDTH), BF),
        pltpu.VMEM((WIDTH, WIDTH), BF),
        pltpu.VMEM((WIDTH, WIDTH), BF),
        pltpu.VMEM((2, 2, WIDTH, ROWS), BF),
        dma((4,)),
        pltpu.VMEM((2, ROWS, WIDTH), F32),
        pltpu.VMEM((2, ROWS, 128), F32),
        pltpu.VMEM((8, ROWS, WIDTH), BF),
        pltpu.VMEM((2, ROWS, WIDTH), BF),
        pltpu.VMEM((2, 8, ROWS, ROWS), BF),
        pltpu.VMEM((8, ROWS, WIDTH), BF),
        pltpu.VMEM((2, 4, ROWS, WIDTH), BF),
        pltpu.VMEM((ROWS, WIDTH), BF),
        pltpu.VMEM((ROWS, WIDTH), BF),
        pltpu.VMEM((ROWS, WIDTH), F32),
        pltpu.VMEM((2, ROWS, WIDTH), BF),
        pltpu.VMEM((2, ROWS, WIDTH), BF),
        pltpu.VMEM((2, ROWS, WIDTH // 2), BF),
        pltpu.VMEM((2, 4, 2, 4, 8, 16, 128), BF),
        pltpu.VMEM((2, 3, 4, 8, 16, 128), BF),
        pltpu.VMEM((2, 3, 4, 8, 16, 128), BF),
        pltpu.VMEM((2, 4, 8, 16, 128), BF),
        pltpu.VMEM((2, 4, 8, 16, 128), BF),
        pltpu.VMEM((2, 3, 8, 16, 128), BF),
        pltpu.VMEM((2, 3, 8, 16, 128), BF),
        pltpu.VMEM((2, 8, 2, 16, 128), BF),
        pltpu.VMEM((2, 7, 2, 16, 128), BF),
        pltpu.VMEM((2, 16, 2, 16, 128), BF),
        dma((2, 4)),
        dma((2, 4, 4)),
        dma((2, 4)),
        dma((2, 4, 4)),
        dma((2,)),
        dma((2,)),
        dma((2, 2)),
        dma((2, 2)),
        dma((2, 2)),
        dma((2, 2)),
        dma((2, 2)),
        dma((2, 2)),
        dma((2, 1)),
        dma((2, 1)),
        dma((2, 1)),
        dma((2, 1)),
    ]
    shapes = (rows, rows, sums, sums)
    vmem = pl.BlockSpec(memory_space=pltpu.VMEM)
    results = pl.pallas_call(
        functools.partial(kernel, groups_rows),
        out_shape=tuple(pltpu.VMEM(v.shape, v.dtype) for v in shapes),
        in_specs=[anywhere] * 4 + [smem] * 3,
        out_specs=(vmem,) * 4,
        scratch_shapes=scratch,
        compiler_params=pltpu.CompilerParams(
            collective_id=0, has_side_effects=True, vmem_limit_bytes=52 * 2**20
        ),
    )(*(
        pltpu.with_memory_space_constraint(v, pltpu.HBM)
        for v in (score_feats[0], audio_feats[0], score_weight, audio_weight)
    ), log_temp, logit_bias, loss_scale)
    back_s, back_a, rows_s, rows_a = pl.pallas_call(
        finish,
        out_shape=shapes,
        in_specs=[vmem] * 4,
        out_specs=(anywhere,) * 4,
        scratch_shapes=[dma((4,))],
    )(*(pltpu.with_memory_space_constraint(v, pltpu.VMEM) for v in results))
    return back_s[None], back_a[None], rows_s, rows_a


def solution(mesh):
    in_specs = (P("dp", "blk", None), P("dp", "blk", None), P(), P(), P(), P(), P())
    out_specs = (P("dp", "blk", None), P("dp", "blk", None), P("blk", None), P("blk", None))
    return jax.shard_map(body, mesh=mesh, in_specs=in_specs, out_specs=out_specs, check_vma=False)
```

```python
import functools

import jax
import jax.numpy as jnp
from jax import lax
from jax.experimental import pallas as pl
from jax.experimental.pallas import tpu as pltpu
from jax.sharding import PartitionSpec as P

MESH = pl.DeviceIdType.MESH
BF = jnp.bfloat16
F32 = jnp.float32
ROWS = 240
WIDTH = 1024
TILE = 256
STEP = 48

LOW = ((0, 64), (64, 48))
HIGH = ((112, 64), (176, 64))
CHUNKS = LOW + HIGH
PLUS, MINUS = 0, 1
GATHER_FAR = {PLUS: HIGH, MINUS: LOW}
GATHER_ORDER = {PLUS: HIGH + LOW, MINUS: LOW + HIGH}
SUM_FAR = {PLUS: LOW, MINUS: HIGH}


def dot_nn(a, b):
    return lax.dot_general(a, b, (((1,), (0,)), ((), ())), preferred_element_type=F32)


def dot_nt(a, b):
    return lax.dot_general(a, b, (((1,), (1,)), ((), ())), preferred_element_type=F32)


def dot_tn(a, b):
    return lax.dot_general(a, b, (((0,), (0,)), ((), ())), preferred_element_type=F32)


def tile_at(index, size):
    return pl.ds(pl.multiple_of(index * size, size), size)


def kernel(
    groups_rows,
    feat_s_in, feat_a_in, weight_s_in, weight_a_in, temp_ref, bias_ref, scale_ref,
    back_s, back_a, rows_s, rows_a,
    feat_s, feat_a, weight_s, weight_a, feat_t,
    load_sem,
    unit, length, audio, score, grad_t, part, ring, side_out, side_in, emb_grad, proj_grad,
    feat_other, proj_other, half, y_in, x_in, y_sum, x_sum, x_in2, y_in2, z_out, z_in, done,
    gather_send, gather_recv, ring_send, ring_recv, side_send, side_recv,
    core_send, core_recv, one_send, one_recv, two_send, two_recv, z_send, z_recv, all_send, all_recv,
):
    blk, dp = lax.axis_index("blk"), lax.axis_index("dp")
    zz, xh = blk // 2, lax.rem(blk, 2)
    xl, yy, core = dp // 8, lax.rem(dp // 2, 4), lax.rem(dp, 2)
    xx = xh * 2 + xl

    def device(dx=0, dy=0, dz=0, dc=0):
        x = lax.rem(xx + dx, 4)
        y = lax.rem(yy + dy, 4)
        z = lax.rem(zz + dz, 8)
        c = lax.rem(core + dc, 2)
        return {"blk": z * 2 + x // 2, "dp": (lax.rem(x, 2) * 4 + y) * 2 + c}

    def flat_dp(offset):
        return {"blk": blk, "dp": lax.rem(dp + offset, 16)}

    def remote(src, dst, send, recv, target):
        return pltpu.make_async_remote_copy(
            src_ref=src, dst_ref=dst, send_sem=send, recv_sem=recv, device_id=target, device_id_type=MESH
        )

    barrier = pltpu.get_barrier_semaphore()
    peers = [device(dz=1), device(dz=7), device(dc=1)]
    peers += [device(dx=k) for k in (2, 1, 3)] + [device(dy=k) for k in (2, 1, 3)]
    for peer in peers:
        pl.semaphore_signal(barrier, inc=1, device_id=peer, device_id_type=MESH)

    loads = [
        pltpu.make_async_copy(src, dst, load_sem.at[i])
        for i, (src, dst) in enumerate((
            (feat_a_in, feat_a), (weight_a_in, weight_a), (feat_s_in, feat_s), (weight_s_in, weight_s),
        ))
    ]
    for copy in loads:
        copy.start()

    temper = jnp.exp(jnp.full((1, 1), temp_ref[0], F32))
    bias = bias_ref[0]
    factor = scale_ref[0] * temper / groups_rows

    def launch(copy):
        copy.start()

    def launch_all(copies):
        for copy in copies:
            copy.start()

    def rows_in(first, count, fn):
        def step(i, carry):
            fn(pl.ds(pl.multiple_of(first + i * 16, 16), 16))
            return carry

        lax.fori_loop(0, count // 16, step, 0, unroll=True)

    def project(tower, feat, weight, store):
        def column(j, carry):
            cols = tile_at(j, TILE)
            unit[tower, :, cols] = dot_nn(feat[...], weight[:, cols])
            return carry

        lax.fori_loop(0, WIDTH // TILE, column, 0)

        def scale(i, carry):
            rows = tile_at(i, STEP)
            value = unit[tower, rows, :]
            norm = jnp.sqrt(jnp.sum(value * value, axis=-1, keepdims=True) + 1e-06)
            value = value / norm
            unit[tower, rows, :] = value
            length[tower, rows, :] = jnp.broadcast_to(norm, (STEP, 128))
            store(rows, value.astype(BF))
            return carry

        lax.fori_loop(0, ROWS // STEP, scale, 0)

    def store_audio(rows, value):
        audio[0, rows, :] = value

    def store_score(rows, value):
        score[0, rows, :] = value

    def gather_copy(way, hop, chunk):
        first, count = chunk
        rows = pl.ds(first, count)
        if way == PLUS:
            here, there = (8 - (hop - 1)) % 8, 8 - hop
        else:
            here, there = hop - 1, hop
        index = CHUNKS.index(chunk)
        return remote(
            audio.at[here, rows], audio.at[there, rows],
            gather_send.at[way, hop - 1], gather_recv.at[way, hop - 1, index],
            device(dz=1 if way == PLUS else 7),
        )

    def ring_slot(way, ahead):
        return ahead if way == PLUS else (8 - ahead) % 8

    def ring_copy(way, hop, chunk):
        first, count = chunk
        rows = pl.ds(first, count)
        start = 0 if chunk in SUM_FAR[way] else 1
        src = part.at[ring_slot(way, 4 - hop), rows] if hop == start else ring.at[way, hop - 1, rows]
        index = CHUNKS.index(chunk)
        return remote(
            src, ring.at[way, hop, rows],
            ring_send.at[way, hop], ring_recv.at[way, hop, index],
            device(dz=1 if way == PLUS else 7),
        )

    def ring_take(way, hop, chunk):
        ring_copy(way, hop, chunk).wait_recv()
        if hop < 3:
            slot = ring_slot(way, 3 - hop)

            def add(rows):
                ring[way, hop, rows, :] = (
                    ring[way, hop, rows, :].astype(F32) + part[slot, rows, :].astype(F32)
                ).astype(BF)

            rows_in(chunk[0], chunk[1], add)
            launch(ring_copy(way, hop + 1, chunk))

    def tile_grads(slot, own):
        for side in range(2):
            logits = temper * dot_nt(audio[slot], score[side]) + bias
            grads = jax.nn.sigmoid(logits)
            if own and side == 0:
                row_ids = lax.broadcasted_iota(jnp.int32, (ROWS, ROWS), 0)
                col_ids = lax.broadcasted_iota(jnp.int32, (ROWS, ROWS), 1)
                grads = grads - (row_ids == col_ids).astype(F32)
            grad_t[side, slot] = grads.astype(BF)

        def column(j, carry):
            cols = tile_at(j, TILE)
            part[slot, :, cols] = (
                dot_nn(grad_t[0, slot], score[0, :, cols]) + dot_nn(grad_t[1, slot], score[1, :, cols])
            ).astype(BF)
            return carry

        lax.fori_loop(0, WIDTH // TILE, column, 0)

    def tile_pair(hop):
        def one(i, carry):
            tile_grads(hop + i * (8 - 2 * hop), False)
            return carry

        lax.fori_loop(0, 2, one, 0)

    def score_grad(side, store, first, count):
        def column(j, carry):
            cols = tile_at(j, TILE)
            total = dot_tn(grad_t[side, 0], audio[0, :, cols])
            for slot in range(1, 8):
                total += dot_tn(grad_t[side, slot], audio[slot, :, cols])
            store(cols, total)
            return carry

        lax.fori_loop(first, first + count, column, 0)

    def unit_grad(tower, value_of, first, count):
        def step(rows):
            grad = factor * value_of(rows)
            vec = unit[tower, rows, :]
            radial = jnp.sum(vec * grad, axis=-1, keepdims=True)
            norm = length[tower, rows, 0:1]
            proj_grad[tower, rows, :] = ((grad - vec * radial) / norm).astype(BF)

        rows_in(first, count, step)

    def back(tower, weight, out):
        def column(j, carry):
            cols = tile_at(j, TILE)
            out[:, cols] = dot_nt(proj_grad[tower], weight[cols, :]).astype(BF)
            return carry

        lax.fori_loop(0, WIDTH // TILE, column, 0)

    def transpose(tower, side, feat):
        def step(z, carry):
            cols = tile_at(z, 128)
            feat_t[tower, side, cols, :] = feat[:, cols].T
            return carry

        lax.fori_loop(0, 8, step, 0)

    def feat_copy(tower, feat):
        return remote(feat, feat_other.at[tower], core_send.at[tower, 0], core_recv.at[tower, 0], device(dc=1))

    def proj_copy(tower, first=0, count=ROWS):
        cols = pl.ds(pl.multiple_of(lax.rem(core + 1, 2) * 512, 512), 512)
        return remote(
            proj_grad.at[tower, pl.ds(first, count), cols], proj_other.at[tower, pl.ds(first, count)],
            core_send.at[tower, 1], core_recv.at[tower, 1], device(dc=1),
        )

    def weight_part(tower, order):
        pair = lax.rem(yy // 2 + 1 + order, 2)
        own_cols = tile_at(core * 2 + pair, 256)
        other_cols = tile_at(pair, 256)

        def step(i, carry):
            rows = tile_at(i, 512)
            value = dot_nn(feat_t[tower, 0, rows, :], proj_grad[tower, :, own_cols])
            value += dot_nn(feat_t[tower, 1, rows, :], proj_other[tower, :, other_cols])
            value = value.astype(BF)
            for z in range(4):
                for q in range(2):
                    for x in range(4):
                        for route in range(2):
                            first = z * 128 + x * 32 + route * 16
                            half[tower, pair * 2 + q, route, x, i * 4 + z] = value[
                                first : first + 16, q * 128 : q * 128 + 128
                            ]
            return carry

        lax.fori_loop(0, 2, step, 0)

    def y_copy(tower, k):
        return remote(
            half.at[tower, lax.rem(yy + k, 4), 0], y_in.at[tower, k - 1],
            one_send.at[tower, 0], one_recv.at[tower, 0], device(dy=k),
        )

    def x_copy(tower, order, k):
        blocks = pl.ds(lax.rem(yy // 2 + 1 + order, 2) * 2, 2)
        return remote(
            half.at[tower, blocks, 1, lax.rem(xx + k, 4)], x_in.at[tower, k - 1, blocks],
            one_send.at[tower, 1], one_recv.at[tower, 1], device(dx=k),
        )

    def launch_some(tower, order):
        launch(x_copy(tower, order, 2))
        if order == 0:
            launch(y_copy(tower, 2))
            launch(y_copy(tower, 3 - 2 * lax.rem(yy, 2)))
        else:
            launch(y_copy(tower, 1 + 2 * lax.rem(yy, 2)))
        launch(x_copy(tower, order, 1))
        launch(x_copy(tower, order, 3))

    def two_copies(tower, route):
        if route == 0:
            return [
                remote(
                    y_sum.at[tower, lax.rem(xx + k, 4)], x_in2.at[tower, k - 1],
                    two_send.at[tower, 0], two_recv.at[tower, 0], device(dx=k),
                )
                for k in (2, 1, 3)
            ]
        return [
            remote(
                x_sum.at[tower, lax.rem(yy + k, 4)], y_in2.at[tower, k - 1],
                two_send.at[tower, 1], two_recv.at[tower, 1], device(dy=k),
            )
            for k in (2, 1, 3)
        ]

    def z_copies(tower):
        return [
            remote(
                z_out.at[tower, lax.rem(zz + k, 8)], z_in.at[tower, k - 1],
                z_send.at[tower, 0], z_recv.at[tower, 0], device(dz=k),
            )
            for k in (4, 3, 5, 2, 6, 1, 7)
        ]

    place = (core * 4 + yy) * 2 + xl

    def all_copies(tower):
        return [
            remote(
                done.at[tower, place], done.at[tower, place],
                all_send.at[tower, 0], all_recv.at[tower, 0], flat_dp(k),
            )
            for k in range(1, 16)
        ]

    def stage_waits(tower, name):
        bufs, send, recv = {
            "one": ((y_in, x_in), one_send, one_recv),
            "two": ((x_in2, y_in2), two_send, two_recv),
            "z": ((z_in,), z_send, z_recv),
            "all": ((done,), all_send, all_recv),
        }[name]
        copies = []
        for i, buf in enumerate(bufs):
            view = buf.at[tower, pl.ds(0, 15)] if name == "all" else buf.at[tower]
            copies.append(remote(view, view, send.at[tower, i], recv.at[tower, i], device(dc=1)))
        return copies

    def stage_one_sum(tower):
        first, second = stage_waits(tower, "one")
        first.wait_recv()

        def y_step(i, carry):
            total = half[tower, yy, 0, i].astype(F32)
            for k in range(3):
                total += y_in[tower, k, i].astype(F32)
            y_sum[tower, i] = total.astype(BF)
            return carry

        lax.fori_loop(0, 4, y_step, 0)
        launch_all(two_copies(tower, 0))
        second.wait_recv()

        def x_step(i, carry):
            total = half[tower, i, 1, xx].astype(F32)
            for k in range(3):
                total += x_in[tower, k, i].astype(F32)
            x_sum[tower, i] = total.astype(BF)
            return carry

        lax.fori_loop(0, 4, x_step, 0)
        launch_all(two_copies(tower, 1))

    def stage_two_sum(tower):
        for copy in stage_waits(tower, "two"):
            copy.wait_recv()
        total = y_sum[tower, xx].astype(F32)
        for k in range(3):
            total += x_in2[tower, k].astype(F32)
        z_out[tower, :, 0] = total.astype(BF)
        total = x_sum[tower, yy].astype(F32)
        for k in range(3):
            total += y_in2[tower, k].astype(F32)
        z_out[tower, :, 1] = total.astype(BF)
        launch_all(z_copies(tower))

    def stage_z_sum(tower):
        for copy in stage_waits(tower, "z"):
            copy.wait_recv()
        total = z_out[tower, zz].astype(F32)
        for k in range(7):
            total += z_in[tower, k].astype(F32)
        done[tower, place] = total.astype(BF)
        launch_all(all_copies(tower))

    def stage_all(tower, out):
        for copy in stage_waits(tower, "all"):
            copy.wait_recv()
        for q in range(8):
            for half_rows in range(2):
                for route in range(2):
                    first = half_rows * 32 + route * 16
                    out[first : first + 16, q * 128 : q * 128 + 128] = done[tower, q * 2 + half_rows, route].astype(F32)

    loads[0].wait()
    loads[1].wait()
    project(1, feat_a, weight_a, store_audio)
    pl.semaphore_wait(barrier, len(peers))
    for i in range(len(CHUNKS)):
        for way in (PLUS, MINUS):
            launch(gather_copy(way, 1, GATHER_ORDER[way][i]))
    loads[2].wait()
    loads[3].wait()
    project(0, feat_s, weight_s, store_score)
    pair = remote(score.at[0], score.at[1], side_send.at[0], side_recv.at[0], device(dx=2))
    launch(pair)
    launch(feat_copy(0, feat_s))
    launch(feat_copy(1, feat_a))
    transpose(0, 0, feat_s)
    transpose(1, 0, feat_a)

    for hop in range(1, 5):
        for i in range(len(CHUNKS)):
            for way in (PLUS, MINUS):
                chunk = GATHER_ORDER[way][i]
                if hop == 4 and chunk not in GATHER_FAR[way]:
                    continue
                gather_copy(way, hop, chunk).wait_recv()
                if hop < 3 or (hop == 3 and chunk in GATHER_FAR[way]):
                    launch(gather_copy(way, hop + 1, chunk))
        if hop == 1:
            pair.wait_recv()
            tile_grads(0, True)
            for tower, feat in enumerate((feat_s, feat_a)):
                feat_copy(tower, feat).wait_recv()
                transpose(tower, 1, feat_other.at[tower])
        if hop < 4:
            tile_pair(hop)
        else:
            tile_grads(4, False)
        if hop >= 3:
            for way in (PLUS, MINUS):
                for chunk in SUM_FAR[way] if hop == 4 else SUM_FAR[1 - way]:
                    launch(ring_copy(way, 4 - hop, chunk))

    def store_side(cols, value):
        side_out[:, cols] = value.astype(BF)

    def store_own(cols, value):
        emb_grad[:, cols] = value

    side = remote(side_out, side_in, side_send.at[1], side_recv.at[1], device(dx=2))
    def own_column(j):
        return lambda: score_grad(0, store_own, j, 1)

    def score_unit():
        side.wait_recv()
        unit_grad(0, lambda rows: emb_grad[rows, :] + side_in[rows, :].astype(F32), 0, ROWS)
        launch(proj_copy(0))

    def score_first():
        proj_copy(0).wait_recv()
        weight_part(0, 0)

    def score_second():
        weight_part(0, 1)
        launch_some(0, 0)
        launch_some(0, 1)

    def score_back():
        back(0, weight_s, back_s)

    beside = {
        0: own_column(0), 1: own_column(1), 2: own_column(2), 3: own_column(3),
        6: score_unit, 7: score_first, 8: score_second, 9: score_back,
        11: lambda: stage_one_sum(0),
    }
    takes = []
    for hop, table, k in (
        (1, 1, 0), (1, 1, 1), (0, 0, 0), (0, 0, 1), (2, 1, 0), (1, 0, 0),
        (1, 0, 1), (2, 1, 1), (3, 1, 0), (2, 0, 0), (2, 0, 1), (3, 1, 1),
    ):
        takes.append([(way, hop, SUM_FAR[way ^ table][k]) for way in (PLUS, MINUS)])

    score_grad(1, store_side, 0, 4)
    launch(side)
    for i, both in enumerate(takes):
        for way, hop, chunk in both:
            ring_take(way, hop, chunk)
        if i in beside:
            beside[i]()

    def audio_value(rows):
        return (
            part[0, rows, :].astype(F32) + ring[PLUS, 3, rows, :].astype(F32) + ring[MINUS, 3, rows, :].astype(F32)
        )

    for k in range(2):
        for way in (PLUS, MINUS):
            ring_take(way, 3, SUM_FAR[way][k])
            unit_grad(1, audio_value, *SUM_FAR[way][k])
            launch(proj_copy(1, *SUM_FAR[way][k]))
    stage_two_sum(0)
    proj_copy(1).wait_recv()
    weight_part(1, 0)
    launch_some(1, 0)
    weight_part(1, 1)
    launch_some(1, 1)
    back(1, weight_a, back_a)
    stage_one_sum(1)
    stage_z_sum(0)
    stage_two_sum(1)
    stage_all(0, rows_s)
    stage_z_sum(1)

    for way in (PLUS, MINUS):
        for hop in range(4):
            for kind in range(2):
                far_rows = (GATHER_FAR, SUM_FAR)[kind][way]
                edge = hop == (3, 0)[kind]
                rows = pl.ds(far_rows[0][0], far_rows[0][1] + far_rows[1][1]) if edge else pl.ds(0, ROWS)
                buf = (audio.at[1, rows], ring.at[way, 1, rows])[kind]
                sem = (gather_send, ring_send)[kind].at[way, hop]
                remote(buf, buf, sem, (gather_recv, ring_recv)[kind].at[way, hop, 0], device(dz=1)).wait_send()
    pair.wait_send()
    side.wait_send()
    for tower in range(2):
        feat_copy(tower, (feat_s, feat_a)[tower]).wait_send()
        proj_copy(tower).wait_send()
        for name in ("one", "two", "z", "all")[: 4 - tower]:
            for copy in stage_waits(tower, name):
                copy.wait_send()
    stage_all(1, rows_a)
    for copy in stage_waits(1, "all"):
        copy.wait_send()


def finish(*refs):
    copies = [pltpu.make_async_copy(refs[i], refs[4 + i], refs[8].at[i]) for i in range(4)]
    for copy in copies:
        copy.start()
    for copy in copies:
        copy.wait()


def body(score_feats, audio_feats, score_weight, audio_weight, log_temp, logit_bias, loss_scale):
    groups_rows = float(lax.axis_size("dp") * lax.axis_size("blk") * score_feats.shape[1])
    anywhere = pl.BlockSpec(memory_space=pl.ANY)
    smem = pl.BlockSpec(memory_space=pltpu.SMEM)
    rows = jax.ShapeDtypeStruct((ROWS, WIDTH), BF)
    sums = jax.ShapeDtypeStruct((64, WIDTH), F32)
    dma = pltpu.SemaphoreType.DMA
    scratch = [
        pltpu.VMEM((ROWS, WIDTH), BF),
        pltpu.VMEM((ROWS, WIDTH), BF),
        pltpu.VMEM((WIDTH, WIDTH), BF),
        pltpu.VMEM((WIDTH, WIDTH), BF),
        pltpu.VMEM((2, 2, WIDTH, ROWS), BF),
        dma((4,)),
        pltpu.VMEM((2, ROWS, WIDTH), F32),
        pltpu.VMEM((2, ROWS, 128), F32),
        pltpu.VMEM((8, ROWS, WIDTH), BF),
        pltpu.VMEM((2, ROWS, WIDTH), BF),
        pltpu.VMEM((2, 8, ROWS, ROWS), BF),
        pltpu.VMEM((8, ROWS, WIDTH), BF),
        pltpu.VMEM((2, 4, ROWS, WIDTH), BF),
        pltpu.VMEM((ROWS, WIDTH), BF),
        pltpu.VMEM((ROWS, WIDTH), BF),
        pltpu.VMEM((ROWS, WIDTH), F32),
        pltpu.VMEM((2, ROWS, WIDTH), BF),
        pltpu.VMEM((2, ROWS, WIDTH), BF),
        pltpu.VMEM((2, ROWS, WIDTH // 2), BF),
        pltpu.VMEM((2, 4, 2, 4, 8, 16, 128), BF),
        pltpu.VMEM((2, 3, 4, 8, 16, 128), BF),
        pltpu.VMEM((2, 3, 4, 8, 16, 128), BF),
        pltpu.VMEM((2, 4, 8, 16, 128), BF),
        pltpu.VMEM((2, 4, 8, 16, 128), BF),
        pltpu.VMEM((2, 3, 8, 16, 128), BF),
        pltpu.VMEM((2, 3, 8, 16, 128), BF),
        pltpu.VMEM((2, 8, 2, 16, 128), BF),
        pltpu.VMEM((2, 7, 2, 16, 128), BF),
        pltpu.VMEM((2, 16, 2, 16, 128), BF),
        dma((2, 4)),
        dma((2, 4, 4)),
        dma((2, 4)),
        dma((2, 4, 4)),
        dma((2,)),
        dma((2,)),
        dma((2, 2)),
        dma((2, 2)),
        dma((2, 2)),
        dma((2, 2)),
        dma((2, 2)),
        dma((2, 2)),
        dma((2, 1)),
        dma((2, 1)),
        dma((2, 1)),
        dma((2, 1)),
    ]
    shapes = (rows, rows, sums, sums)
    vmem = pl.BlockSpec(memory_space=pltpu.VMEM)
    results = pl.pallas_call(
        functools.partial(kernel, groups_rows),
        out_shape=tuple(pltpu.VMEM(v.shape, v.dtype) for v in shapes),
        in_specs=[anywhere] * 4 + [smem] * 3,
        out_specs=(vmem,) * 4,
        scratch_shapes=scratch,
        compiler_params=pltpu.CompilerParams(
            collective_id=0, has_side_effects=True, vmem_limit_bytes=52 * 2**20
        ),
    )(*(
        pltpu.with_memory_space_constraint(v, pltpu.HBM)
        for v in (score_feats[0], audio_feats[0], score_weight, audio_weight)
    ), log_temp, logit_bias, loss_scale)
    back_s, back_a, rows_s, rows_a = pl.pallas_call(
        finish,
        out_shape=shapes,
        in_specs=[vmem] * 4,
        out_specs=(anywhere,) * 4,
        scratch_shapes=[dma((4,))],
    )(*(pltpu.with_memory_space_constraint(v, pltpu.VMEM) for v in results))
    return back_s[None], back_a[None], rows_s, rows_a


def solution(mesh):
    in_specs = (P("dp", "blk", None), P("dp", "blk", None), P(), P(), P(), P(), P())
    out_specs = (P("dp", "blk", None), P("dp", "blk", None), P("blk", None), P("blk", None))
    return jax.shard_map(body, mesh=mesh, in_specs=in_specs, out_specs=out_specs, check_vma=False)
```
